32 devices in a mesh: grp: 4 (over y, core), lane: 8 (over z, x).
Axes of the slice: x: 2, y: 2, z: 4, core: 2. Of those that a mesh axis runs over, the one named last changes fastest.
Arguments:
- fine_in: bfloat16 [2, 512, 16, 256], P(None, ('grp', 'lane')), may hold values from -6 to 6
- counts: int32 [2, 32], P(None, ('grp', 'lane')), may hold values from 1 to 15, as said below
- neighbour_refs: int32 [2, 512, 16], P(None, ('grp', 'lane')), may hold values from 0 to 79, as said below
- offset_codes: int32 [2, 512, 16], P(None, ('grp', 'lane')), may hold values from 0 to 26, as said below
- neighbour_mask: int32 [2, 512, 16], P(None, ('grp', 'lane')), may hold values 0 or 1
- send_slots: int32 [2, 32, 64], P(None, ('grp', 'lane')), may hold values from 0 to 14, as said below
- parent_of: int32 [512], P(('grp', 'lane')), may hold values from -1 to 7, as said below
- child_code: int32 [512], P(('grp', 'lane')), may hold values from 0 to 7, as said below
- coarse_refs: int32 [32, 16], P(('grp', 'lane')), may hold values from 0 to 31
- coarse_codes: int32 [32, 16], P(('grp', 'lane')), may hold values from 0 to 26, as said below
- coarse_mask: int32 [32, 16], P(('grp', 'lane')), may hold values 0 or 1
- ops_x: bfloat16 [3, 4, 3, 16, 16], replicated, may hold values from -0.75 to 0.75
- ops_y: bfloat16 [3, 4, 3, 16, 16], replicated, may hold values from -0.75 to 0.75
- ops_z: bfloat16 [3, 4, 3, 16, 16], replicated, may hold values from -0.75 to 0.75
- filters: bfloat16 [2, 16, 16], replicated, may hold values from -1.5 to 1.5
Outputs:
- fine_out: bfloat16 [2, 512, 16, 256], P(None, ('grp', 'lane'))
- coarse_out: bfloat16 [32, 16, 256], P(('grp', 'lane'))
The draws below stay inside these ranges and needn't reach their ends.
Inputs may be any that keep to these rules, and one draw needn't show every extreme that they name: The counts of the devices of one grp index add up to 64 on level 1. send_slots[l, q, r * 2 + c] is a live slot of device q on level l. `neighbour_refs`: A value below 16 is a live slot of the block's own device; a larger one is 16 + q * 2 + c, entry c of what device q sends to the block's device. `offset_codes`: the codes of one block are distinct. `coarse_codes`: the codes of one coarse block are distinct. `parent_of`: -1 exactly on slots that are not live on level 1; every coarse block of a subtree has 8 live children there, one of each child code. `child_code`: 0 on slots that are not live.
All inputs are finite; a program needn't handle non-finite values. No bound on the sum of `neighbour_mask` or of `coarse_mask` on one device may be relied on, other than what follows from the above.
Results may differ from the reference program's by a relative error of at most 0.0088.
Values may be sent and summed in bfloat16 or wider, within the bound.
A program may use at most 256 MiB of HBM per device.

```python
import jax
import jax.numpy as jnp
from jax import lax

K = 16
TERMS = 4
NB = 16
PAR_LANE = 1
CAP = 2
SLOT = 16
BLOCKS = 512
PAR_GRP = 8
PAR = 32
N_GRP = 4
N_LANE = 8
DEVICES = 32


def live_counts(key, level_index):
    pair_count = DEVICES // 2
    middle = 8 * PAR_LANE
    spread = jax.random.randint(jax.random.fold_in(key, 101 + level_index), (pair_count,), 0, middle)
    spread = jnp.where(jnp.arange(pair_count, dtype=jnp.int32) == 0, middle - 1, spread)
    return jnp.stack([middle + spread, middle - spread], axis=1).reshape(DEVICES).astype(jnp.int32)


def distinct_codes(key, row_total):
    scores = jax.random.randint(key, (row_total, 27), 0, 1 << 20) * 32 + jnp.arange(27, dtype=jnp.int32)[None, :]
    ordering = jnp.argsort(scores, axis=1)
    return ordering[:, :NB].astype(jnp.int32)


def neighbour_table(key, level_index):
    counts_level = live_counts(key, level_index)
    slot_ids = jnp.arange(BLOCKS, dtype=jnp.int32)
    local_count = counts_level[slot_ids // SLOT][:, None]
    keys = jax.random.split(jax.random.fold_in(key, 201 + level_index), 3)
    own_slot = jax.random.randint(keys[0], (BLOCKS, NB), 0, 1 << 20) % local_count
    far_slot = SLOT + jax.random.randint(keys[1], (BLOCKS, NB), 0, DEVICES * CAP)
    choose_far = jax.random.randint(keys[2], (BLOCKS, NB), 0, 2)
    return jnp.where(choose_far == 1, far_slot, own_slot).astype(jnp.int32)


def send_table(key, level_index):
    counts_level = live_counts(key, level_index)
    raw_slots = jax.random.randint(jax.random.fold_in(key, 601 + level_index), (DEVICES, DEVICES * CAP), 0, 1 << 20)
    return (raw_slots % counts_level[:, None]).astype(jnp.int32)


def family(key):
    counts_one = live_counts(key, 1)
    slot_ids = jnp.arange(BLOCKS, dtype=jnp.int32)
    live_mask = slot_ids % SLOT < counts_one[slot_ids // SLOT]
    flags = live_mask.astype(jnp.int32).reshape(N_GRP, SLOT * N_LANE)
    ranks = jnp.cumsum(flags, axis=1) - 1
    children = 8 * PAR_LANE * N_LANE
    scores = jax.random.randint(jax.random.fold_in(key, 301), (N_GRP, children), 0, 1 << 18) * 4096 + jnp.arange(children, dtype=jnp.int32)[None, :]
    ordering = jnp.argsort(scores, axis=1).astype(jnp.int32)
    position = jnp.take_along_axis(ordering, jnp.maximum(ranks, 0), axis=1).reshape(BLOCKS)
    parent = jnp.where(live_mask, position // 8, -1).astype(jnp.int32)
    code_value = jnp.where(live_mask, position % 8, 0).astype(jnp.int32)
    return (parent, code_value)


def draw_counts(key, part):
    return jnp.stack([live_counts(key, 0), live_counts(key, 1)])


def draw_neighbour_refs(key, part):
    return jnp.stack([neighbour_table(key, 0), neighbour_table(key, 1)])


def draw_offset_codes(key, part):
    return jnp.stack([distinct_codes(jax.random.fold_in(key, 401), BLOCKS), distinct_codes(jax.random.fold_in(key, 402), BLOCKS)])


def draw_send_slots(key, part):
    return jnp.stack([send_table(key, 0), send_table(key, 1)])


def draw_parent_of(key, part):
    return family(key)[0]


def draw_child_code(key, part):
    return family(key)[1]


def draw_coarse_codes(key, part):
    return distinct_codes(jax.random.fold_in(key, 501), PAR)


def place_ends(values, key, least, largest):
    place = [jax.random.randint(jax.random.fold_in(key, axis), (), 0, length) for axis, length in enumerate(values.shape)]
    main_axis = values.shape.index(max(values.shape))
    next_to = place[:main_axis] + [(place[main_axis] + 1) % values.shape[main_axis]] + place[main_axis + 1:]
    return values.at[tuple(place)].set(least).at[tuple(next_to)].set(largest)


def steps_of(own_key, extent, cuts, low, high):
    def one(dim, parts):
        steps = jax.random.uniform(jax.random.fold_in(jax.random.fold_in(own_key, 6), dim), (parts,), jnp.float32, low / len(cuts), high / len(cuts))
        return jnp.repeat(jnp.exp(steps), extent[dim] // parts).reshape((-1,) + (1,) * (len(extent) - dim - 1))

    factor_of = one(*cuts[0])
    for cut in cuts[1:]:
        factor_of = factor_of * one(*cut)
    return factor_of


def bell_draw(stream_key, extent, scale, most, shards=(), kind=jnp.bfloat16):
    loudness = steps_of(stream_key, extent, shards, -0.22, 0.18) if shards else 1.0
    array = jax.random.normal(stream_key, extent, jnp.float32) * scale * loudness
    return jnp.minimum(jnp.maximum(array, -most), most).astype(kind)


def setup_inputs(seed: int = 0) -> dict:
    key_of = jax.random.split(jax.random.key(seed), 16)
    return {
        "fine_in": bell_draw(key_of[0], (2, BLOCKS, K, K * K), 1.0, 6.0, ((1, 32),)),
        "counts": draw_counts(jax.random.fold_in(key_of[15], 71), 0),
        "neighbour_refs": draw_neighbour_refs(jax.random.fold_in(key_of[15], 71), 0),
        "offset_codes": draw_offset_codes(jax.random.fold_in(key_of[15], 71), 0),
        "neighbour_mask": place_ends((jax.random.randint(key_of[4], (2, BLOCKS, NB), 0, 4) < 3).astype(jnp.int32), jax.random.fold_in(key_of[4], 1), 0, 1),
        "send_slots": draw_send_slots(jax.random.fold_in(key_of[15], 71), 0),
        "parent_of": draw_parent_of(jax.random.fold_in(key_of[15], 71), 0),
        "child_code": draw_child_code(jax.random.fold_in(key_of[15], 71), 0),
        "coarse_refs": place_ends(jax.random.randint(key_of[8], (PAR, NB), 0, PAR), jax.random.fold_in(key_of[8], 1), 0, PAR - 1).astype(jnp.int32),
        "coarse_codes": draw_coarse_codes(jax.random.fold_in(key_of[15], 71), 0),
        "coarse_mask": place_ends((jax.random.randint(key_of[10], (PAR, NB), 0, 4) < 3).astype(jnp.int32), jax.random.fold_in(key_of[10], 1), 0, 1),
        "ops_x": bell_draw(key_of[11], (3, TERMS, 3, K, K), (4 * K) ** -0.5, 0.75),
        "ops_y": bell_draw(key_of[12], (3, TERMS, 3, K, K), (4 * K) ** -0.5, 0.75),
        "ops_z": bell_draw(key_of[13], (3, TERMS, 3, K, K), (4 * K) ** -0.5, 0.75),
        "filters": bell_draw(key_of[14], (2, K, K), K ** -0.5, 1.5),
    }


offset_total = 27


def kron_tables(left_ops, right_ops):
    first = left_ops.astype(jnp.float32)[:, :, None, :, None, :, None]
    second = right_ops.astype(jnp.float32)[:, None, :, None, :, None, :]
    order_size = left_ops.shape[-1]
    product_full = first * second
    return product_full.reshape(-1, order_size * order_size, order_size * order_size).astype(jnp.bfloat16)


def apply_blocks(source_blocks, offset_codes, neighbour_mask, row_ops, tables):
    row_count = source_blocks.shape[0]
    order_size = source_blocks.shape[2]
    select = ((offset_codes[:, :, None] == jnp.arange(offset_total, dtype=jnp.int32)[None, None, :]) & (neighbour_mask[:, :, None] == 1)).astype(jnp.float32)
    grouped = jnp.einsum("bjc,bjxy->bcxy", select, source_blocks.astype(jnp.float32)).astype(jnp.bfloat16)
    grouped = grouped.reshape(row_count, 3, 9, order_size, order_size * order_size)
    spread = jnp.einsum("mapq,bacqr->bmcpr", row_ops.astype(jnp.float32), grouped.astype(jnp.float32)).astype(jnp.bfloat16)
    spread = spread.reshape(row_count, -1, order_size, order_size * order_size)
    return jnp.einsum("bcpr,csr->bps", spread.astype(jnp.float32), tables.astype(jnp.float32))


def corner_sum(lifted_rows, filter_tables, corner, transpose):
    block_count = corner.shape[0]
    running = jnp.zeros(lifted_rows.shape, jnp.float32)
    for corner_index in range(4):
        filter_table = filter_tables[corner_index].T if transpose else filter_tables[corner_index]
        product = jnp.dot(lifted_rows, filter_table, preferred_element_type=jnp.float32)
        chosen = jnp.repeat(corner == corner_index, lifted_rows.shape[0] // block_count)[:, None]
        running = running + jnp.where(chosen, product, jnp.zeros_like(product))
    return running.reshape(block_count, -1, lifted_rows.shape[1])


def source_index(neighbour_refs, send_slots):
    owner = (jnp.arange(neighbour_refs.shape[0], dtype=jnp.int32) // SLOT)[:, None]
    far_entry = jnp.maximum(neighbour_refs - SLOT, 0)
    peer_index = far_entry // CAP
    sent_slot = send_slots[peer_index, owner * CAP + far_entry % CAP]
    return jnp.where(neighbour_refs < SLOT, owner * SLOT + neighbour_refs, peer_index * SLOT + sent_slot).astype(jnp.int32)


def fine_level(blocks, counts, neighbour_refs, offset_codes, neighbour_mask, send_slots, row_ops, tables):
    slot_ids = jnp.arange(blocks.shape[0], dtype=jnp.int32)
    live_mask = (slot_ids % SLOT) < counts[slot_ids // SLOT]
    masked = jnp.where(live_mask[:, None, None], blocks, jnp.zeros_like(blocks))
    anchor = source_index(neighbour_refs, send_slots)

    def one_device(pieces):
        anchor_rows, code_rows, mask_rows = pieces
        return apply_blocks(masked[anchor_rows], code_rows, mask_rows, row_ops, tables)

    def shaped(values):
        return values.reshape(DEVICES, SLOT, -1)

    result = lax.map(one_device, (shaped(anchor), shaped(offset_codes), shaped(neighbour_mask)))
    result = result.reshape(blocks.shape[0], blocks.shape[1], blocks.shape[2])
    return jnp.where(live_mask[:, None, None], result, jnp.zeros_like(result)), live_mask, masked


def reference(fine_in, counts, neighbour_refs, offset_codes, neighbour_mask, send_slots, parent_of, child_code, coarse_refs, coarse_codes, coarse_mask, ops_x, ops_y, ops_z, filters):
    fine_terms = []
    masked_levels = []
    live_levels = []
    for level_index in range(2):
        tables = kron_tables(ops_y[level_index], ops_z[level_index])
        result, live_mask, masked = fine_level(fine_in[level_index], counts[level_index], neighbour_refs[level_index], offset_codes[level_index], neighbour_mask[level_index], send_slots[level_index], ops_x[level_index], tables)
        fine_terms.append(result)
        masked_levels.append(masked)
        live_levels.append(live_mask)
    filter_tables = kron_tables(filters[None], filters[None])
    upper_bit = child_code // 4
    corner = child_code % 4
    flat = masked_levels[1].astype(jnp.float32)
    lower_lift = jnp.einsum("pq,bqr->bpr", filters[0].astype(jnp.float32), flat)
    upper_lift = jnp.einsum("pq,bqr->bpr", filters[1].astype(jnp.float32), flat)
    lifted = jnp.where((upper_bit == 0)[:, None, None], lower_lift, upper_lift).astype(jnp.bfloat16)
    sibling_term = corner_sum(lifted.reshape(-1, K * K), filter_tables, corner, True)
    slot_ids = jnp.arange(parent_of.shape[0], dtype=jnp.int32)
    parent_global = (slot_ids // (SLOT * N_LANE)) * PAR_GRP + jnp.maximum(parent_of, 0)
    coarse_in = jax.ops.segment_sum(sibling_term, parent_global, num_segments=PAR).astype(jnp.bfloat16)
    coarse_tables = kron_tables(ops_y[2], ops_z[2])

    def one_coarse(pieces):
        ref_rows, code_rows, mask_rows = pieces
        return apply_blocks(coarse_in[ref_rows], code_rows, mask_rows, ops_x[2], coarse_tables)

    coarse_full = lax.map(one_coarse, (coarse_refs.reshape(DEVICES, PAR_LANE, -1), coarse_codes.reshape(DEVICES, PAR_LANE, -1), coarse_mask.reshape(DEVICES, PAR_LANE, -1)))
    coarse_out = coarse_full.reshape(PAR, K, K * K).astype(jnp.bfloat16)
    picked = jnp.where(live_levels[1][:, None, None], coarse_out[parent_global], jnp.zeros((parent_of.shape[0], K, K * K), jnp.bfloat16))
    flat_picked = picked.astype(jnp.float32)
    lower_drop = jnp.einsum("qp,bqr->bpr", filters[0].astype(jnp.float32), flat_picked)
    upper_drop = jnp.einsum("qp,bqr->bpr", filters[1].astype(jnp.float32), flat_picked)
    lowered = jnp.where((upper_bit == 0)[:, None, None], lower_drop, upper_drop).astype(jnp.bfloat16)
    correction = corner_sum(lowered.reshape(-1, K * K), filter_tables, corner, False)
    fine_one = fine_terms[1] + correction
    fine_out = jnp.stack([fine_terms[0], fine_one]).astype(jnp.bfloat16)
    return fine_out, coarse_out
```

```python
import functools

import jax
import jax.numpy as jnp
from jax import lax
from jax.experimental import pallas as pl
from jax.experimental.pallas import tpu as pltpu
from jax.sharding import PartitionSpec as P

MESH = pl.DeviceIdType.MESH
BF = jnp.bfloat16
F32 = jnp.float32
OFFSETS = 27
PLANES = 9
GROUP = 4


def dot_nn(a, b):
    return jnp.dot(a, b, preferred_element_type=F32)


def dot_nt(a, b):
    return lax.dot_general(a, b, (((1,), (1,)), ((), ())), preferred_element_type=F32)


def one_hot(shape, fn):
    rows = lax.broadcasted_iota(jnp.int32, shape, 0)
    cols = lax.broadcasted_iota(jnp.int32, shape, 1)
    return jnp.where(fn(rows, cols), 1.0, 0.0).astype(BF)


def spread_first(k):
    return one_hot((k, k * k), lambda i, j: (j >= i * k) & (j < i * k + k))


def spread_second(k):
    return one_hot((k, k * k), lambda i, j: lax.rem(j, k) == i)


def kron_rows(left, right, k):
    return jnp.concatenate([(left[p : p + 1, :] * right).astype(BF) for p in range(k)], axis=0)


def build_filters(filters_ref, hk_ref, k):
    first, second = spread_first(k), spread_second(k)
    left = [dot_nn(filters_ref[c], first) for c in range(2)]
    right = [dot_nn(filters_ref[c], second) for c in range(2)]
    for cy in range(2):
        for cz in range(2):
            hk_ref[2 * cy + cz] = kron_rows(left[cy], right[cz], k)


def build_tables(level, ops_y_ref, ops_z_ref, kr_ref, k, terms):
    first, second = spread_first(k), spread_second(k)

    def one_term(m, carry):
        right = [dot_nn(ops_z_ref[level, m, c], second) for c in range(3)]
        for cy in range(3):
            left = dot_nn(ops_y_ref[level, m, cy], first)
            for cz in range(3):
                kr_ref[m * PLANES + 3 * cy + cz] = kron_rows(left, right[cz], k)
        return carry

    lax.fori_loop(0, terms, one_term, 0)


def build_rows(level, ops_x_ref, group, k, terms):
    width = group * 3 * k
    blocks = []
    stacked = [
        jnp.concatenate([ops_x_ref[level, m, c] for m in range(terms)], axis=0) for c in range(3)
    ]
    for g in range(group):
        total = None
        for c in range(3):
            offset = (g * 3 + c) * k
            part = dot_nn(stacked[c], one_hot((k, width), lambda i, j: j == i + offset))
            total = part if total is None else total + part
        blocks.append(total.astype(BF))
    return jnp.concatenate(
        [blocks[g][m * k : (m + 1) * k] for m in range(terms) for g in range(group)], axis=0
    )


def spread_group(base, group, rows_mat, load, s_ref, k, terms):
    for plane in range(PLANES):
        source = jnp.concatenate(
            [load(base + g, 9 * c + plane) for g in range(group) for c in range(3)], axis=0
        )
        out = dot_nn(rows_mat, source).astype(BF)
        span = group * k
        for m in range(terms):
            s_ref[m * PLANES + plane, pl.ds(base * k, span), :] = out[m * span : (m + 1) * span]


def apply_tables(s_ref, kr_ref, rows, k, terms):
    def one_term(m, total):
        for plane in range(PLANES):
            at = m * PLANES + plane
            total = total + dot_nt(s_ref[at, pl.ds(0, rows), :], kr_ref[at])
        return total

    return lax.fori_loop(0, terms, one_term, jnp.zeros((rows, k * k), F32))


def comm_kernel(
    dims,
    fine_ref,
    slots_ref,
    parent_ref,
    child_ref,
    cidx_ref,
    ops_x_ref,
    ops_y_ref,
    ops_z_ref,
    filters_ref,
    pool_out,
    group_out,
    coarse_out,
    pool,
    outgoing,
    partial,
    rs_buf,
    coarse_all,
    group_all,
    hk,
    kr,
    s_buf,
    wide,
    send_rs,
    recv_rs,
    send_ag,
    recv_ag,
    send_co,
    recv_co,
    send_fine,
    recv_fine,
):
    n_grp, n_lane, cap, slot, par_lane, k, terms = dims
    n_dev = n_grp * n_lane
    grp = lax.axis_index("grp")
    lane = lax.axis_index("lane")
    me = grp * n_lane + lane

    def coords(d):
        return (lax.div(d, n_lane), lax.rem(d, n_lane))

    barrier = pltpu.get_barrier_semaphore()

    def greet(i, carry):
        pl.semaphore_signal(
            barrier, inc=1, device_id=coords(lax.rem(me + i, n_dev)), device_id_type=MESH
        )
        return carry

    lax.fori_loop(1, n_dev, greet, 0)

    build_filters(filters_ref, hk, k)
    both = jnp.concatenate([filters_ref[0], filters_ref[1]], axis=0)
    for b in range(slot):
        lifted = dot_nn(both, fine_ref[1, b])
        code = child_ref[b]
        upper = code >= 4
        corner = jnp.where(upper, code - 4, code)
        chosen = jnp.where(upper, lifted[k:], lifted[:k])
        for c in range(4):
            wide[c, b * k : (b + 1) * k, :] = jnp.where(corner == c, chosen, 0.0).astype(BF)
    terms_up = dot_nt(wide[0], hk[0])
    for c in range(1, 4):
        terms_up = terms_up + dot_nt(wide[c], hk[c])
    for t in range(n_lane * par_lane):
        total = jnp.zeros((k, k * k), F32)
        for b in range(slot):
            total = total + jnp.where(parent_ref[b] == t, terms_up[b * k : (b + 1) * k], 0.0)
        partial[t // par_lane, t % par_lane] = total

    def gather(d, carry):
        for level in range(2):
            for c in range(cap):
                outgoing[level, d, c] = fine_ref[level, slots_ref[level, 0, d * cap + c]]
        return carry

    lax.fori_loop(0, n_dev, gather, 0)
    pl.semaphore_wait(barrier, n_dev - 1)

    def send_partial(i, carry):
        to = lax.rem(lane + i, n_lane)
        pltpu.make_async_remote_copy(
            src_ref=partial.at[to],
            dst_ref=rs_buf.at[lane],
            send_sem=send_rs,
            recv_sem=recv_rs,
            device_id=(grp, to),
            device_id_type=MESH,
        ).start()
        return carry

    lax.fori_loop(1, n_lane, send_partial, 0)

    def send_fine_level(level):
        def one(i, carry):
            d = lax.rem(me + i, n_dev)
            pltpu.make_async_remote_copy(
                src_ref=outgoing.at[level, d],
                dst_ref=pool.at[level, pl.ds(slot + me * cap, cap)],
                send_sem=send_fine.at[level],
                recv_sem=recv_fine.at[level],
                device_id=coords(d),
                device_id_type=MESH,
            ).start()
            return carry

        lax.fori_loop(1, n_dev, one, 0)

    rs_buf[lane] = partial[lane]
    for level in range(2):
        pool[level, pl.ds(0, slot)] = fine_ref[level]
        pool[level, pl.ds(slot + me * cap, cap)] = outgoing[level, me]
        pool[level, slot + n_dev * cap] = jnp.zeros((k, k * k), BF)
    coarse_all[n_dev * par_lane] = jnp.zeros((k, k * k), BF)
    build_tables(2, ops_y_ref, ops_z_ref, kr, k, terms)
    rows_mat = build_rows(2, ops_x_ref, 1, k, terms)

    def await_bytes(ref, sem):
        pltpu.make_async_copy(ref, ref, sem).wait()

    await_bytes(rs_buf.at[pl.ds(0, n_lane - 1)], recv_rs)
    total = rs_buf[0]
    for t in range(1, n_lane):
        total = total + rs_buf[t]
    coarse_all[pl.ds(me * par_lane, par_lane)] = total.astype(BF)

    def send_coarse(i, carry):
        d = lax.rem(me + i, n_dev)
        mine = coarse_all.at[pl.ds(me * par_lane, par_lane)]
        pltpu.make_async_remote_copy(
            src_ref=mine,
            dst_ref=mine,
            send_sem=send_ag,
            recv_sem=recv_ag,
            device_id=coords(d),
            device_id_type=MESH,
        ).start()
        return carry

    lax.fori_loop(1, n_dev, send_coarse, 0)
    send_fine_level(0)
    send_fine_level(1)
    await_bytes(coarse_all.at[pl.ds(0, (n_dev - 1) * par_lane)], recv_ag)

    for b in range(par_lane):
        spread_group(
            b, 1, rows_mat, lambda i, code: coarse_all[cidx_ref[i, code]], s_buf, k, terms
        )
    result = apply_tables(s_buf, kr, par_lane * k, k, terms).astype(BF)
    for b in range(par_lane):
        group_all[lane, b] = result[b * k : (b + 1) * k]
        coarse_out[b] = result[b * k : (b + 1) * k]

    def send_result(i, carry):
        to = lax.rem(lane + i, n_lane)
        pltpu.make_async_remote_copy(
            src_ref=group_all.at[lane],
            dst_ref=group_all.at[lane],
            send_sem=send_co,
            recv_sem=recv_co,
            device_id=(grp, to),
            device_id_type=MESH,
        ).start()
        return carry

    lax.fori_loop(1, n_lane, send_result, 0)
    await_bytes(group_all.at[pl.ds(0, n_lane - 1)], recv_co)
    group_out[...] = group_all[...]
    for level in range(2):
        await_bytes(pool.at[level, pl.ds(0, (n_dev - 1) * cap)], recv_fine.at[level])
    pool_out[...] = pool[...]
    await_bytes(rs_buf.at[pl.ds(0, n_lane - 1)], send_rs)
    await_bytes(coarse_all.at[pl.ds(0, (n_dev - 1) * par_lane)], send_ag)
    await_bytes(group_all.at[pl.ds(0, n_lane - 1)], send_co)
    for level in range(2):
        await_bytes(pool.at[level, pl.ds(0, (n_dev - 1) * cap)], send_fine.at[level])


def fine_kernel(
    dims,
    pool,
    group_all,
    idx_ref,
    counts_ref,
    parent_ref,
    child_ref,
    ops_x_ref,
    ops_y_ref,
    ops_z_ref,
    filters_ref,
    out_ref,
    hk,
    kr,
    s_buf,
    wide,
):
    n_grp, n_lane, cap, slot, par_lane, k, terms = dims
    build_filters(filters_ref, hk, k)
    correction = drop(group_all, parent_ref, child_ref, filters_ref, hk, wide, slot, par_lane, k)
    for level in range(2):
        build_tables(level, ops_y_ref, ops_z_ref, kr, k, terms)
        result = fine_operator(level, pool, idx_ref, ops_x_ref, kr, s_buf, slot, k, terms)
        for b in range(slot):
            value = jnp.where(b < counts_ref[level, 0], result[b * k : (b + 1) * k], 0.0)
            if level == 1:
                value = value + correction[b * k : (b + 1) * k]
            out_ref[level, b] = value.astype(BF)


def fine_operator(level, pool, idx_ref, ops_x_ref, kr, s_buf, slot, k, terms):
    group = GROUP if slot % GROUP == 0 else 1
    rows_mat = build_rows(level, ops_x_ref, group, k, terms)

    def one_group(g, carry):
        spread_group(
            pl.multiple_of(g * group, group),
            group,
            rows_mat,
            lambda i, code: pool[level, idx_ref[level, i, code]],
            s_buf,
            k,
            terms,
        )
        return carry

    lax.fori_loop(0, slot // group, one_group, 0)
    return apply_tables(s_buf, kr, slot * k, k, terms)


def drop(group_all, parent_ref, child_ref, filters_ref, hk, wide, slot, par_lane, k):
    eye = one_hot((k, k), lambda i, j: i == j)
    both = jnp.concatenate([dot_nt(eye, filters_ref[c]).astype(BF) for c in range(2)], axis=0)
    for b in range(slot):
        parent = parent_ref[b]
        held = jnp.maximum(parent, 0)
        lowered = dot_nn(both, group_all[held])
        code = child_ref[b]
        upper = code >= 4
        corner = jnp.where(upper, code - 4, code)
        corner = jnp.where(parent >= 0, corner, -1)
        chosen = jnp.where(upper, lowered[k:], lowered[:k])
        for c in range(4):
            wide[c, b * k : (b + 1) * k, :] = jnp.where(corner == c, chosen, 0.0).astype(BF)
    total = dot_nn(wide[0], hk[0])
    for c in range(1, 4):
        total = total + dot_nn(wide[c], hk[c])
    return total


def code_table(refs, codes, mask, empty):
    hits = (
        codes[..., None, :] == jnp.arange(OFFSETS, dtype=jnp.int32)[:, None]
    ) & (mask[..., None, :] == 1)
    return empty + jnp.sum(jnp.where(hits, refs[..., None, :] - empty, 0), axis=-1)


def body(
    fine_in,
    counts,
    neighbour_refs,
    offset_codes,
    neighbour_mask,
    send_slots,
    parent_of,
    child_code,
    coarse_refs,
    coarse_codes,
    coarse_mask,
    ops_x,
    ops_y,
    ops_z,
    filters,
):
    n_grp, n_lane = lax.axis_size("grp"), lax.axis_size("lane")
    n_dev = n_grp * n_lane
    k = filters.shape[1]
    kk = k * k
    slot = fine_in.shape[1]
    cap = send_slots.shape[2] // n_dev
    par_lane = coarse_refs.shape[0]
    terms = ops_x.shape[1]
    dims = (n_grp, n_lane, cap, slot, par_lane, k, terms)
    pool_size = slot + n_dev * cap + 1
    idx = code_table(neighbour_refs, offset_codes, neighbour_mask, slot + n_dev * cap)
    cidx = code_table(coarse_refs, coarse_codes, coarse_mask, n_dev * par_lane)
    vmem = pl.BlockSpec(memory_space=pltpu.VMEM)
    smem = pl.BlockSpec(memory_space=pltpu.SMEM)
    pool, group_all, coarse_out = pl.pallas_call(
        functools.partial(comm_kernel, dims),
        out_shape=(
            jax.ShapeDtypeStruct((2, pool_size, k, kk), BF),
            jax.ShapeDtypeStruct((n_lane, par_lane, k, kk), BF),
            jax.ShapeDtypeStruct((par_lane, k, kk), BF),
        ),
        in_specs=[vmem, smem, smem, smem, smem, vmem, vmem, vmem, vmem],
        out_specs=(vmem, vmem, vmem),
        scratch_shapes=[
            pltpu.VMEM((2, pool_size, k, kk), BF),
            pltpu.VMEM((2, n_dev, cap, k, kk), BF),
            pltpu.VMEM((n_lane, par_lane, k, kk), F32),
            pltpu.VMEM((n_lane, par_lane, k, kk), F32),
            pltpu.VMEM((n_dev * par_lane + 1, k, kk), BF),
            pltpu.VMEM((n_lane, par_lane, k, kk), BF),
            pltpu.VMEM((4, kk, kk), BF),
            pltpu.VMEM((terms * PLANES, kk, kk), BF),
            pltpu.VMEM((terms * PLANES, par_lane * k, kk), BF),
            pltpu.VMEM((4, slot * k, kk), BF),
            pltpu.SemaphoreType.DMA,
            pltpu.SemaphoreType.DMA,
            pltpu.SemaphoreType.DMA,
            pltpu.SemaphoreType.DMA,
            pltpu.SemaphoreType.DMA,
            pltpu.SemaphoreType.DMA,
            pltpu.SemaphoreType.DMA((2,)),
            pltpu.SemaphoreType.DMA((2,)),
        ],
        compiler_params=pltpu.CompilerParams(
            collective_id=0, has_side_effects=True, vmem_limit_bytes=48 * 1024 * 1024
        ),
    )(fine_in, send_slots, parent_of, child_code, cidx, ops_x, ops_y, ops_z, filters)
    fine_out = pl.pallas_call(
        functools.partial(fine_kernel, dims),
        out_shape=jax.ShapeDtypeStruct(fine_in.shape, BF),
        in_specs=[vmem, vmem, smem, smem, smem, smem, vmem, vmem, vmem, vmem],
        out_specs=vmem,
        scratch_shapes=[
            pltpu.VMEM((4, kk, kk), BF),
            pltpu.VMEM((terms * PLANES, kk, kk), BF),
            pltpu.VMEM((terms * PLANES, slot * k, kk), BF),
            pltpu.VMEM((4, slot * k, kk), BF),
        ],
        compiler_params=pltpu.CompilerParams(vmem_limit_bytes=48 * 1024 * 1024),
    )(
        pool,
        group_all.reshape(n_lane * par_lane, k, kk),
        idx,
        counts,
        parent_of,
        child_code,
        ops_x,
        ops_y,
        ops_z,
        filters,
    )
    return fine_out, coarse_out


def solution(mesh):
    both = ("grp", "lane")
    in_specs = (
        P(None, both, None, None),
        P(None, both),
        P(None, both, None),
        P(None, both, None),
        P(None, both, None),
        P(None, both, None),
        P(both),
        P(both),
        P(both, None),
        P(both, None),
        P(both, None),
        P(),
        P(),
        P(),
        P(),
    )
    out_specs = (P(None, both, None, None), P(both, None, None))
    return jax.shard_map(body, mesh=mesh, in_specs=in_specs, out_specs=out_specs, check_vma=False)
```

```python
import functools

import jax
import jax.numpy as jnp
from jax import lax
from jax.experimental import pallas as pl
from jax.experimental.pallas import tpu as pltpu
from jax.sharding import PartitionSpec as P

MESH = pl.DeviceIdType.MESH
BF = jnp.bfloat16
F32 = jnp.float32
OFFSETS = 27
PLANES = 9
GROUP = 4


def dot_nn(a, b):
    return jnp.dot(a, b, preferred_element_type=F32)


def dot_nt(a, b):
    return lax.dot_general(a, b, (((1,), (1,)), ((), ())), preferred_element_type=F32)


def one_hot(shape, fn):
    rows = lax.broadcasted_iota(jnp.int32, shape, 0)
    cols = lax.broadcasted_iota(jnp.int32, shape, 1)
    return jnp.where(fn(rows, cols), 1.0, 0.0).astype(BF)


def spread_first(k):
    return one_hot((k, k * k), lambda i, j: (j >= i * k) & (j < i * k + k))


def spread_second(k):
    return one_hot((k, k * k), lambda i, j: lax.rem(j, k) == i)


def kron_rows(left, right, k):
    return jnp.concatenate([(left[p : p + 1, :] * right).astype(BF) for p in range(k)], axis=0)


def build_filters(filters_ref, hk_ref, k):
    first, second = spread_first(k), spread_second(k)
    left = [dot_nn(filters_ref[c], first) for c in range(2)]
    right = [dot_nn(filters_ref[c], second) for c in range(2)]
    for cy in range(2):
        for cz in range(2):
            hk_ref[2 * cy + cz] = kron_rows(left[cy], right[cz], k)


def build_tables(level, ops_y_ref, ops_z_ref, kr_ref, k, terms):
    first, second = spread_first(k), spread_second(k)

    def one_term(m, carry):
        right = [dot_nn(ops_z_ref[level, m, c], second) for c in range(3)]
        for cy in range(3):
            left = dot_nn(ops_y_ref[level, m, cy], first)
            for cz in range(3):
                kr_ref[m * PLANES + 3 * cy + cz] = kron_rows(left, right[cz], k)
        return carry

    lax.fori_loop(0, terms, one_term, 0)


def build_rows(level, ops_x_ref, group, k, terms):
    width = group * 3 * k
    blocks = []
    stacked = [
        jnp.concatenate([ops_x_ref[level, m, c] for m in range(terms)], axis=0) for c in range(3)
    ]
    for g in range(group):
        total = None
        for c in range(3):
            offset = (g * 3 + c) * k
            part = dot_nn(stacked[c], one_hot((k, width), lambda i, j: j == i + offset))
            total = part if total is None else total + part
        blocks.append(total.astype(BF))
    return jnp.concatenate(
        [blocks[g][m * k : (m + 1) * k] for m in range(terms) for g in range(group)], axis=0
    )


def spread_group(base, group, rows_mat, load, s_ref, k, terms):
    for plane in range(PLANES):
        source = jnp.concatenate(
            [load(base + g, 9 * c + plane) for g in range(group) for c in range(3)], axis=0
        )
        out = dot_nn(rows_mat, source).astype(BF)
        span = group * k
        for m in range(terms):
            s_ref[m * PLANES + plane, pl.ds(base * k, span), :] = out[m * span : (m + 1) * span]


def apply_tables(s_ref, kr_ref, rows, k, terms):
    def one_term(m, total):
        for plane in range(PLANES):
            at = m * PLANES + plane
            total = total + dot_nt(s_ref[at, pl.ds(0, rows), :], kr_ref[at])
        return total

    return lax.fori_loop(0, terms, one_term, jnp.zeros((rows, k * k), F32))


def fill_index(refs, codes, mask, empty, out_ref, at):
    rows, slots = refs.shape
    code_of = lax.broadcasted_iota(jnp.int32, (rows, 128), 1)
    total = jnp.full((rows, 128), empty, jnp.int32)
    for j in range(slots):
        hit = (codes[:, j : j + 1] == code_of) & (mask[:, j : j + 1] == 1)
        total = jnp.where(hit, refs[:, j : j + 1], total)
    out_ref[at] = total


def tree_kernel(
    dims,
    fine_hbm,
    counts_hbm,
    refs_hbm,
    codes_hbm,
    mask_hbm,
    slots_hbm,
    parent_hbm,
    child_hbm,
    crefs_hbm,
    ccodes_hbm,
    cmask_hbm,
    ops_x_hbm,
    ops_y_hbm,
    ops_z_hbm,
    filters_hbm,
    out_ref,
    coarse_out,
    counts_ref,
    refs_ref,
    codes_ref,
    mask_ref,
    slots_ref,
    parent_ref,
    child_ref,
    crefs_ref,
    ccodes_ref,
    cmask_ref,
    ops_x_ref,
    ops_y_ref,
    ops_z_ref,
    filters_ref,
    idx_vec,
    cidx_vec,
    idx_ref,
    cidx_ref,
    own_0,
    own_1,
    pool_0,
    pool_1,
    outgoing,
    partial,
    rs_buf,
    coarse_all,
    group_all,
    hk,
    kr,
    s_buf,
    wide,
    in_sems,
    send_rs,
    recv_rs,
    send_ag,
    recv_ag,
    send_co,
    recv_co,
    send_fine,
    recv_fine,
):
    n_grp, n_lane, cap, slot, par_lane, k, terms = dims
    n_dev = n_grp * n_lane
    own, pool = (own_0, own_1), (pool_0, pool_1)
    grp = lax.axis_index("grp")
    lane = lax.axis_index("lane")
    me = grp * n_lane + lane

    def coords(d):
        return (lax.div(d, n_lane), lax.rem(d, n_lane))

    fetches = [
        pltpu.make_async_copy(src, dst, in_sems.at[i])
        for i, (src, dst) in enumerate(
            [
                (filters_hbm, filters_ref),
                (fine_hbm.at[1], own_1),
                (child_hbm, child_ref),
                (parent_hbm, parent_ref),
                (slots_hbm, slots_ref),
                (fine_hbm.at[0], own_0),
                (crefs_hbm, crefs_ref),
                (ccodes_hbm, ccodes_ref),
                (cmask_hbm, cmask_ref),
                (ops_x_hbm, ops_x_ref),
                (ops_y_hbm, ops_y_ref),
                (ops_z_hbm, ops_z_ref),
                (refs_hbm, refs_ref),
                (codes_hbm, codes_ref),
                (mask_hbm, mask_ref),
                (counts_hbm, counts_ref),
            ]
        )
    ]
    for fetch in fetches:
        fetch.start()

    barrier = pltpu.get_barrier_semaphore()

    def greet(i, carry):
        pl.semaphore_signal(
            barrier, inc=1, device_id=coords(lax.rem(me + i, n_dev)), device_id_type=MESH
        )
        return carry

    lax.fori_loop(1, n_dev, greet, 0)

    for fetch in fetches[:4]:
        fetch.wait()
    build_filters(filters_ref, hk, k)
    both = jnp.concatenate([filters_ref[0], filters_ref[1]], axis=0)
    for b in range(slot):
        lifted = dot_nn(both, own_1[b])
        code = child_ref[b]
        upper = code >= 4
        corner = jnp.where(upper, code - 4, code)
        chosen = jnp.where(upper, lifted[k:], lifted[:k])
        for c in range(4):
            wide[c, b * k : (b + 1) * k, :] = jnp.where(corner == c, chosen, 0.0).astype(BF)
    terms_up = dot_nt(wide[0], hk[0])
    for c in range(1, 4):
        terms_up = terms_up + dot_nt(wide[c], hk[c])
    for t in range(n_lane * par_lane):
        total = jnp.zeros((k, k * k), F32)
        for b in range(slot):
            total = total + jnp.where(parent_ref[b] == t, terms_up[b * k : (b + 1) * k], 0.0)
        partial[t // par_lane, t % par_lane] = total
    pl.semaphore_wait(barrier, n_dev - 1)

    def send_partial(i, carry):
        to = lax.rem(lane + i, n_lane)
        pltpu.make_async_remote_copy(
            src_ref=partial.at[to],
            dst_ref=rs_buf.at[lane],
            send_sem=send_rs,
            recv_sem=recv_rs,
            device_id=(grp, to),
            device_id_type=MESH,
        ).start()
        return carry

    lax.fori_loop(1, n_lane, send_partial, 0)

    def send_fine_level(level):
        def one(i, carry):
            d = lax.rem(me + i, n_dev)
            for c in range(cap):
                outgoing[level, d, c] = own[level][slots_ref[level, 0, d * cap + c]]
            pltpu.make_async_remote_copy(
                src_ref=outgoing.at[level, d],
                dst_ref=pool[level].at[pl.ds(slot + me * cap, cap)],
                send_sem=send_fine.at[level],
                recv_sem=recv_fine.at[level],
                device_id=coords(d),
                device_id_type=MESH,
            ).start()
            return carry

        lax.fori_loop(1, n_dev, one, 0)
        for c in range(cap):
            pool[level][slot + me * cap + c] = own[level][slots_ref[level, 0, me * cap + c]]
        pool[level][slot + n_dev * cap] = jnp.zeros((k, k * k), BF)
        pool[level][pl.ds(0, slot)] = own[level][...]

    for fetch in fetches[4:6]:
        fetch.wait()
    send_fine_level(0)

    rs_buf[lane] = partial[lane]
    coarse_all[n_dev * par_lane] = jnp.zeros((k, k * k), BF)
    for fetch in fetches[6:]:
        fetch.wait()
    fill_index(crefs_ref[...], ccodes_ref[...], cmask_ref[...], n_dev * par_lane, cidx_vec, ...)
    for level in range(2):
        fill_index(
            refs_ref[level], codes_ref[level], mask_ref[level], slot + n_dev * cap, idx_vec, level
        )
    table_copies = [
        pltpu.make_async_copy(cidx_vec, cidx_ref, in_sems.at[0]),
        pltpu.make_async_copy(idx_vec, idx_ref, in_sems.at[1]),
    ]
    for copy in table_copies:
        copy.start()

    def await_bytes(ref, sem):
        pltpu.make_async_copy(ref, ref, sem).wait()

    await_bytes(rs_buf.at[pl.ds(0, n_lane - 1)], recv_rs)
    total = rs_buf[0]
    for t in range(1, n_lane):
        total = total + rs_buf[t]
    coarse_all[pl.ds(me * par_lane, par_lane)] = total.astype(BF)

    def send_coarse(i, carry):
        d = lax.rem(me + i, n_dev)
        mine = coarse_all.at[pl.ds(me * par_lane, par_lane)]
        pltpu.make_async_remote_copy(
            src_ref=mine,
            dst_ref=mine,
            send_sem=send_ag,
            recv_sem=recv_ag,
            device_id=coords(d),
            device_id_type=MESH,
        ).start()
        return carry

    lax.fori_loop(1, n_dev, send_coarse, 0)
    send_fine_level(1)
    for level in (2, 0, 1):
        build_tables(level, ops_y_ref, ops_z_ref, kr.at[level], k, terms)
    rows_mat = build_rows(2, ops_x_ref, 1, k, terms)
    for copy in table_copies:
        copy.wait()

    await_bytes(coarse_all.at[pl.ds(0, (n_dev - 1) * par_lane)], recv_ag)
    for b in range(par_lane):
        spread_group(
            b, 1, rows_mat, lambda i, code: coarse_all[cidx_ref[i, code]], s_buf, k, terms
        )
    result = apply_tables(s_buf, kr.at[2], par_lane * k, k, terms).astype(BF)
    for b in range(par_lane):
        group_all[lane, b] = result[b * k : (b + 1) * k]
        coarse_out[b] = result[b * k : (b + 1) * k]

    def send_result(i, carry):
        to = lax.rem(lane + i, n_lane)
        pltpu.make_async_remote_copy(
            src_ref=group_all.at[lane],
            dst_ref=group_all.at[lane],
            send_sem=send_co,
            recv_sem=recv_co,
            device_id=(grp, to),
            device_id_type=MESH,
        ).start()
        return carry

    lax.fori_loop(1, n_lane, send_result, 0)

    await_bytes(pool_0.at[pl.ds(0, (n_dev - 1) * cap)], recv_fine.at[0])
    result = fine_operator(0, pool_0, idx_ref, ops_x_ref, kr.at[0], s_buf, slot, k, terms)
    for b in range(slot):
        value = jnp.where(b < counts_ref[0], result[b * k : (b + 1) * k], 0.0)
        out_ref[0, b] = value.astype(BF)

    await_bytes(group_all.at[pl.ds(0, n_lane - 1)], recv_co)
    correction = drop(
        group_all, parent_ref, child_ref, filters_ref, hk, wide, slot, par_lane, k
    )
    await_bytes(pool_1.at[pl.ds(0, (n_dev - 1) * cap)], recv_fine.at[1])
    result = fine_operator(1, pool_1, idx_ref, ops_x_ref, kr.at[1], s_buf, slot, k, terms)
    for b in range(slot):
        value = jnp.where(b < counts_ref[1], result[b * k : (b + 1) * k], 0.0)
        out_ref[1, b] = (value + correction[b * k : (b + 1) * k]).astype(BF)

    await_bytes(rs_buf.at[pl.ds(0, n_lane - 1)], send_rs)
    await_bytes(coarse_all.at[pl.ds(0, (n_dev - 1) * par_lane)], send_ag)
    await_bytes(group_all.at[pl.ds(0, n_lane - 1)], send_co)
    for level in range(2):
        await_bytes(pool[level].at[pl.ds(0, (n_dev - 1) * cap)], send_fine.at[level])


def fine_operator(level, pool, idx_ref, ops_x_ref, kr, s_buf, slot, k, terms):
    group = GROUP if slot % GROUP == 0 else 1
    rows_mat = build_rows(level, ops_x_ref, group, k, terms)

    def one_group(g, carry):
        spread_group(
            pl.multiple_of(g * group, group),
            group,
            rows_mat,
            lambda i, code: pool[idx_ref[level, i, code]],
            s_buf,
            k,
            terms,
        )
        return carry

    lax.fori_loop(0, slot // group, one_group, 0)
    return apply_tables(s_buf, kr, slot * k, k, terms)


def drop(group_all, parent_ref, child_ref, filters_ref, hk, wide, slot, par_lane, k):
    eye = one_hot((k, k), lambda i, j: i == j)
    both = jnp.concatenate([dot_nt(eye, filters_ref[c]).astype(BF) for c in range(2)], axis=0)
    for b in range(slot):
        parent = parent_ref[b]
        held = jnp.maximum(parent, 0)
        lowered = dot_nn(both, group_all[held // par_lane, held % par_lane] if par_lane > 1 else group_all[held, 0])
        code = child_ref[b]
        upper = code >= 4
        corner = jnp.where(upper, code - 4, code)
        corner = jnp.where(parent >= 0, corner, -1)
        chosen = jnp.where(upper, lowered[k:], lowered[:k])
        for c in range(4):
            wide[c, b * k : (b + 1) * k, :] = jnp.where(corner == c, chosen, 0.0).astype(BF)
    total = dot_nn(wide[0], hk[0])
    for c in range(1, 4):
        total = total + dot_nn(wide[c], hk[c])
    return total


def body(
    fine_in,
    counts,
    neighbour_refs,
    offset_codes,
    neighbour_mask,
    send_slots,
    parent_of,
    child_code,
    coarse_refs,
    coarse_codes,
    coarse_mask,
    ops_x,
    ops_y,
    ops_z,
    filters,
):
    n_grp, n_lane = lax.axis_size("grp"), lax.axis_size("lane")
    n_dev = n_grp * n_lane
    k = filters.shape[1]
    kk = k * k
    slot = fine_in.shape[1]
    cap = send_slots.shape[2] // n_dev
    par_lane = coarse_refs.shape[0]
    terms = ops_x.shape[1]
    dims = (n_grp, n_lane, cap, slot, par_lane, k, terms)
    pool_size = slot + n_dev * cap + 1
    int32 = jnp.int32
    vmem = pl.BlockSpec(memory_space=pltpu.VMEM)
    hbm = pl.BlockSpec(memory_space=pl.ANY)
    dma = pltpu.SemaphoreType.DMA
    return pl.pallas_call(
        functools.partial(tree_kernel, dims),
        out_shape=(
            jax.ShapeDtypeStruct(fine_in.shape, BF),
            jax.ShapeDtypeStruct((par_lane, k, kk), BF),
        ),
        in_specs=[hbm] * 15,
        out_specs=(vmem, vmem),
        scratch_shapes=[
            pltpu.SMEM((2,), int32),
            pltpu.VMEM(neighbour_refs.shape, int32),
            pltpu.VMEM(offset_codes.shape, int32),
            pltpu.VMEM(neighbour_mask.shape, int32),
            pltpu.SMEM(send_slots.shape, int32),
            pltpu.SMEM(parent_of.shape, int32),
            pltpu.SMEM(child_code.shape, int32),
            pltpu.VMEM(coarse_refs.shape, int32),
            pltpu.VMEM(coarse_codes.shape, int32),
            pltpu.VMEM(coarse_mask.shape, int32),
            pltpu.VMEM(ops_x.shape, BF),
            pltpu.VMEM(ops_y.shape, BF),
            pltpu.VMEM(ops_z.shape, BF),
            pltpu.VMEM(filters.shape, BF),
            pltpu.VMEM((2, slot, 128), int32),
            pltpu.VMEM((par_lane, 128), int32),
            pltpu.SMEM((2, slot, 128), int32),
            pltpu.SMEM((par_lane, 128), int32),
            pltpu.VMEM((slot, k, kk), BF),
            pltpu.VMEM((slot, k, kk), BF),
            pltpu.VMEM((pool_size, k, kk), BF),
            pltpu.VMEM((pool_size, k, kk), BF),
            pltpu.VMEM((2, n_dev, cap, k, kk), BF),
            pltpu.VMEM((n_lane, par_lane, k, kk), F32),
            pltpu.VMEM((n_lane, par_lane, k, kk), F32),
            pltpu.VMEM((n_dev * par_lane + 1, k, kk), BF),
            pltpu.VMEM((n_lane, par_lane, k, kk), BF),
            pltpu.VMEM((4, kk, kk), BF),
            pltpu.VMEM((3, terms * PLANES, kk, kk), BF),
            pltpu.VMEM((terms * PLANES, slot * k, kk), BF),
            pltpu.VMEM((4, slot * k, kk), BF),
            dma((16,)),
            dma,
            dma,
            dma,
            dma,
            dma,
            dma,
            dma((2,)),
            dma((2,)),
        ],
        compiler_params=pltpu.CompilerParams(
            collective_id=0, has_side_effects=True, vmem_limit_bytes=56 * 1024 * 1024
        ),
    )(
        fine_in,
        counts.reshape(-1),
        neighbour_refs,
        offset_codes,
        neighbour_mask,
        send_slots,
        parent_of,
        child_code,
        coarse_refs,
        coarse_codes,
        coarse_mask,
        ops_x,
        ops_y,
        ops_z,
        filters,
    )


def solution(mesh):
    both = ("grp", "lane")
    in_specs = (
        P(None, both, None, None),
        P(None, both),
        P(None, both, None),
        P(None, both, None),
        P(None, both, None),
        P(None, both, None),
        P(both),
        P(both),
        P(both, None),
        P(both, None),
        P(both, None),
        P(),
        P(),
        P(),
        P(),
    )
    out_specs = (P(None, both, None, None), P(both, None, None))
    return jax.shard_map(body, mesh=mesh, in_specs=in_specs, out_specs=out_specs, check_vma=False)
```

```python
import functools

import jax
import jax.numpy as jnp
from jax import lax
from jax.experimental import pallas as pl
from jax.experimental.pallas import tpu as pltpu
from jax.sharding import PartitionSpec as P

MESH = pl.DeviceIdType.MESH
BF = jnp.bfloat16
F32 = jnp.float32
OFFSETS = 27
PLANES = 9
GROUP = 4


def dot_nn(a, b):
    return jnp.dot(a, b, preferred_element_type=F32)


def dot_nt(a, b):
    return lax.dot_general(a, b, (((1,), (1,)), ((), ())), preferred_element_type=F32)


def one_hot(shape, fn):
    rows = lax.broadcasted_iota(jnp.int32, shape, 0)
    cols = lax.broadcasted_iota(jnp.int32, shape, 1)
    return jnp.where(fn(rows, cols), 1.0, 0.0).astype(BF)


def spread_first(k):
    return one_hot((k, k * k), lambda i, j: (j >= i * k) & (j < i * k + k))


def spread_second(k):
    return one_hot((k, k * k), lambda i, j: lax.rem(j, k) == i)


def kron_rows(left, right, k):
    return jnp.concatenate([(left[p : p + 1, :] * right).astype(BF) for p in range(k)], axis=0)


def build_filters(filters_ref, hk_ref, k):
    first, second = spread_first(k), spread_second(k)
    left = [dot_nn(filters_ref[c], first) for c in range(2)]
    right = [dot_nn(filters_ref[c], second) for c in range(2)]
    for cy in range(2):
        for cz in range(2):
            hk_ref[2 * cy + cz] = kron_rows(left[cy], right[cz], k)


def build_tables(level, ops_y_ref, ops_z_ref, kr_ref, k, terms):
    first, second = spread_first(k), spread_second(k)
    eye = one_hot((k, k), lambda i, j: i == j)
    kk = k * k

    def turned(matrix):
        return dot_nt(eye, matrix).astype(BF)

    def one_term(m, carry):
        right = [dot_nn(turned(ops_z_ref[level, m, c]), second) for c in range(3)]
        for cy in range(3):
            left = dot_nn(turned(ops_y_ref[level, m, cy]), first)
            for cz in range(3):
                at = (3 * cy + cz) * kk
                kr_ref[m, at : at + kk, :] = kron_rows(left, right[cz], k)
        return carry

    lax.fori_loop(0, terms, one_term, 0)


def build_rows(level, ops_x_ref, group, k, terms):
    width = group * 3 * k
    blocks = []
    stacked = [
        jnp.concatenate([ops_x_ref[level, m, c] for m in range(terms)], axis=0) for c in range(3)
    ]
    for g in range(group):
        total = None
        for c in range(3):
            offset = (g * 3 + c) * k
            part = dot_nn(stacked[c], one_hot((k, width), lambda i, j: j == i + offset))
            total = part if total is None else total + part
        blocks.append(total.astype(BF))
    return jnp.concatenate(
        [blocks[g][m * k : (m + 1) * k] for m in range(terms) for g in range(group)], axis=0
    )


def spread_group(base, group, rows_mat, load, s_ref, k, terms):
    for plane in range(PLANES):
        source = jnp.concatenate(
            [load(base + g, 9 * c + plane) for g in range(group) for c in range(3)], axis=0
        )
        out = dot_nn(rows_mat, source).astype(BF)
        span = group * k
        for m in range(terms):
            s_ref[m, pl.ds(base * k, span), plane * k * k : (plane + 1) * k * k] = out[
                m * span : (m + 1) * span
            ]


def apply_tables(s_ref, kr_ref, rows, k, terms):
    def one_term(m, total):
        return total + dot_nn(s_ref[m, pl.ds(0, rows), :], kr_ref[m])

    return lax.fori_loop(0, terms, one_term, jnp.zeros((rows, k * k), F32))


def fill_index(refs, codes, mask, empty, out_ref, at):
    rows, slots = refs.shape
    code_of = lax.broadcasted_iota(jnp.int32, (rows, 128), 1)
    total = jnp.full((rows, 128), empty, jnp.int32)
    for j in range(slots):
        hit = (codes[:, j : j + 1] == code_of) & (mask[:, j : j + 1] == 1)
        total = jnp.where(hit, refs[:, j : j + 1], total)
    out_ref[at] = total


def tree_kernel(
    dims,
    fine_hbm,
    counts_hbm,
    refs_hbm,
    codes_hbm,
    mask_hbm,
    slots_hbm,
    parent_hbm,
    child_hbm,
    crefs_hbm,
    ccodes_hbm,
    cmask_hbm,
    ops_x_hbm,
    ops_y_hbm,
    ops_z_hbm,
    filters_hbm,
    out_ref,
    coarse_out,
    counts_ref,
    refs_ref,
    codes_ref,
    mask_ref,
    slots_ref,
    parent_ref,
    child_ref,
    crefs_ref,
    ccodes_ref,
    cmask_ref,
    ops_x_ref,
    ops_y_ref,
    ops_z_ref,
    filters_ref,
    idx_vec,
    cidx_vec,
    idx_ref,
    cidx_ref,
    own_0,
    own_1,
    pool_0,
    pool_1,
    outgoing,
    partial,
    rs_buf,
    coarse_all,
    group_all,
    hk,
    kr,
    s_buf,
    wide,
    in_sems,
    send_rs,
    recv_rs,
    send_ag,
    recv_ag,
    send_pass,
    recv_pass,
    send_co,
    recv_co,
    send_fine_sem,
    recv_fine,
):
    n_grp, n_lane, cap, slot, par_lane, k, terms = dims
    n_dev = n_grp * n_lane
    own, pool = (own_0, own_1), (pool_0, pool_1)
    grp = lax.axis_index("grp")
    lane = lax.axis_index("lane")
    me = grp * n_lane + lane

    def coords(d):
        return (lax.div(d, n_lane), lax.rem(d, n_lane))

    barrier = pltpu.get_barrier_semaphore()

    def greet(i, carry):
        pl.semaphore_signal(
            barrier, inc=1, device_id=coords(lax.rem(me + i, n_dev)), device_id_type=MESH
        )
        return carry

    fetches = [
        pltpu.make_async_copy(src, dst, in_sems.at[i])
        for i, (src, dst) in enumerate(
            [
                (slots_hbm, slots_ref),
                (fine_hbm.at[0], own_0),
                (filters_hbm, filters_ref),
                (fine_hbm.at[1], own_1),
                (child_hbm, child_ref),
                (parent_hbm, parent_ref),
                (crefs_hbm, crefs_ref),
                (ccodes_hbm, ccodes_ref),
                (cmask_hbm, cmask_ref),
                (ops_x_hbm, ops_x_ref),
                (ops_y_hbm, ops_y_ref),
                (ops_z_hbm, ops_z_ref),
                (refs_hbm, refs_ref),
                (codes_hbm, codes_ref),
                (mask_hbm, mask_ref),
                (counts_hbm, counts_ref),
            ]
        )
    ]
    for fetch in fetches:
        fetch.start()
    lax.fori_loop(1, n_dev, greet, 0)

    def gather_level(level):
        def one(d, carry):
            for c in range(cap):
                outgoing[level, d, c] = own[level][slots_ref[level, 0, d * cap + c]]
            return carry

        lax.fori_loop(0, n_dev, one, 0)

    def send_fine(level, start, stop):
        def one(i, carry):
            d = lax.rem(me + i, n_dev)
            pltpu.make_async_remote_copy(
                src_ref=outgoing.at[level, d],
                dst_ref=pool[level].at[pl.ds(slot + me * cap, cap)],
                send_sem=send_fine_sem.at[level],
                recv_sem=recv_fine.at[level],
                device_id=coords(d),
                device_id_type=MESH,
            ).start()
            return carry

        lax.fori_loop(start, stop, one, 0)

    def keep_own(level):
        pool[level][pl.ds(slot + me * cap, cap)] = outgoing[level, me]
        pool[level][slot + n_dev * cap] = jnp.zeros((k, k * k), BF)
        pool[level][pl.ds(0, slot)] = own[level][...]

    for fetch in fetches[:2]:
        fetch.wait()
    gather_level(0)
    pl.semaphore_wait(barrier, n_dev - 1)
    send_fine(0, 1, n_dev)

    for fetch in fetches[2:6]:
        fetch.wait()
    build_filters(filters_ref, hk, k)
    both = jnp.concatenate([filters_ref[0], filters_ref[1]], axis=0)
    for b in range(slot):
        lifted = dot_nn(both, own_1[b])
        code = child_ref[b]
        upper = code >= 4
        corner = jnp.where(upper, code - 4, code)
        chosen = jnp.where(upper, lifted[k:], lifted[:k])
        for c in range(4):
            wide[c, b * k : (b + 1) * k, :] = jnp.where(corner == c, chosen, 0.0).astype(BF)
    terms_up = dot_nt(wide[0], hk[0])
    for c in range(1, 4):
        terms_up = terms_up + dot_nt(wide[c], hk[c])
    for t in range(n_lane * par_lane):
        total = jnp.zeros((k, k * k), F32)
        for b in range(slot):
            total = total + jnp.where(parent_ref[b] == t, terms_up[b * k : (b + 1) * k], 0.0)
        partial[t // par_lane, t % par_lane] = total

    def send_partial(i, carry):
        to = lax.rem(lane + i, n_lane)
        pltpu.make_async_remote_copy(
            src_ref=partial.at[to],
            dst_ref=rs_buf.at[lane],
            send_sem=send_rs,
            recv_sem=recv_rs,
            device_id=(grp, to),
            device_id_type=MESH,
        ).start()
        return carry

    lax.fori_loop(1, n_lane, send_partial, 0)
    gather_level(1)
    send_fine(1, 1, n_dev // 2)

    rs_buf[lane] = partial[lane]
    coarse_all[n_dev * par_lane] = jnp.zeros((k, k * k), BF)
    keep_own(0)
    keep_own(1)
    for fetch in fetches[6:]:
        fetch.wait()
    fill_index(crefs_ref[...], ccodes_ref[...], cmask_ref[...], n_dev * par_lane, cidx_vec, ...)
    for level in range(2):
        fill_index(
            refs_ref[level], codes_ref[level], mask_ref[level], slot + n_dev * cap, idx_vec, level
        )
    table_copies = [
        pltpu.make_async_copy(cidx_vec, cidx_ref, in_sems.at[0]),
        pltpu.make_async_copy(idx_vec, idx_ref, in_sems.at[1]),
    ]
    for copy in table_copies:
        copy.start()
    build_tables(0, ops_y_ref, ops_z_ref, kr.at[0], k, terms)

    def await_bytes(ref, sem):
        pltpu.make_async_copy(ref, ref, sem).wait()

    await_bytes(rs_buf.at[pl.ds(0, n_lane - 1)], recv_rs)
    total = rs_buf[0]
    for t in range(1, n_lane):
        total = total + rs_buf[t]
    coarse_all[pl.ds(me * par_lane, par_lane)] = total.astype(BF)

    half = n_dev // 2
    odd = lax.rem(grp, 2)
    twin = grp + 1 - 2 * odd

    def send_coarse(i, carry):
        at = lax.rem(lax.div(grp, 2) * n_lane + lane + i, half)
        mine = coarse_all.at[pl.ds(me * par_lane, par_lane)]
        pltpu.make_async_remote_copy(
            src_ref=mine,
            dst_ref=mine,
            send_sem=send_ag,
            recv_sem=recv_ag,
            device_id=(2 * lax.div(at, n_lane) + odd, lax.rem(at, n_lane)),
            device_id_type=MESH,
        ).start()
        return carry

    lax.fori_loop(1, half, send_coarse, 0)
    send_fine(1, n_dev // 2, n_dev)
    for level in (2, 1):
        build_tables(level, ops_y_ref, ops_z_ref, kr.at[level], k, terms)
    for copy in table_copies:
        copy.wait()

    await_bytes(pool_0.at[pl.ds(0, (n_dev - 1) * cap)], recv_fine.at[0])
    result = fine_operator(0, pool_0, idx_ref, ops_x_ref, kr.at[0], s_buf, slot, k, terms)
    for b in range(slot):
        value = jnp.where(b < counts_ref[0], result[b * k : (b + 1) * k], 0.0)
        out_ref[0, b] = value.astype(BF)

    await_bytes(coarse_all.at[pl.ds(0, (half - 1) * par_lane)], recv_ag)
    for pair in range(n_grp // 2):
        held = coarse_all.at[pl.ds((2 * pair + odd) * n_lane * par_lane, n_lane * par_lane)]
        pltpu.make_async_remote_copy(
            src_ref=held,
            dst_ref=held,
            send_sem=send_pass,
            recv_sem=recv_pass,
            device_id=(twin, lane),
            device_id_type=MESH,
        ).start()
    rows_mat = build_rows(2, ops_x_ref, 1, k, terms)
    await_bytes(coarse_all.at[pl.ds(0, half * par_lane)], recv_pass)
    for b in range(par_lane):
        spread_group(
            b, 1, rows_mat, lambda i, code: coarse_all[cidx_ref[i, code]], s_buf, k, terms
        )
    result = apply_tables(s_buf, kr.at[2], par_lane * k, k, terms).astype(BF)
    for b in range(par_lane):
        group_all[lane, b] = result[b * k : (b + 1) * k]
        coarse_out[b] = result[b * k : (b + 1) * k]

    def send_result(i, carry):
        to = lax.rem(lane + i, n_lane)
        pltpu.make_async_remote_copy(
            src_ref=group_all.at[lane],
            dst_ref=group_all.at[lane],
            send_sem=send_co,
            recv_sem=recv_co,
            device_id=(grp, to),
            device_id_type=MESH,
        ).start()
        return carry

    lax.fori_loop(1, n_lane, send_result, 0)

    await_bytes(pool_1.at[pl.ds(0, (n_dev - 1) * cap)], recv_fine.at[1])
    result = fine_operator(1, pool_1, idx_ref, ops_x_ref, kr.at[1], s_buf, slot, k, terms)
    await_bytes(group_all.at[pl.ds(0, n_lane - 1)], recv_co)
    correction = drop(
        group_all, parent_ref, child_ref, filters_ref, hk, wide, slot, par_lane, k
    )
    for b in range(slot):
        value = jnp.where(b < counts_ref[1], result[b * k : (b + 1) * k], 0.0)
        out_ref[1, b] = (value + correction[b * k : (b + 1) * k]).astype(BF)

    await_bytes(rs_buf.at[pl.ds(0, n_lane - 1)], send_rs)
    await_bytes(coarse_all.at[pl.ds(0, (half - 1) * par_lane)], send_ag)
    await_bytes(coarse_all.at[pl.ds(0, half * par_lane)], send_pass)
    await_bytes(group_all.at[pl.ds(0, n_lane - 1)], send_co)
    for level in range(2):
        await_bytes(pool[level].at[pl.ds(0, (n_dev - 1) * cap)], send_fine_sem.at[level])


def fine_operator(level, pool, idx_ref, ops_x_ref, kr, s_buf, slot, k, terms):
    group = GROUP if slot % GROUP == 0 else 1
    rows_mat = build_rows(level, ops_x_ref, group, k, terms)

    def one_group(g, carry):
        spread_group(
            pl.multiple_of(g * group, group),
            group,
            rows_mat,
            lambda i, code: pool[idx_ref[level, i, code]],
            s_buf,
            k,
            terms,
        )
        return carry

    lax.fori_loop(0, slot // group, one_group, 0)
    return apply_tables(s_buf, kr, slot * k, k, terms)


def drop(group_all, parent_ref, child_ref, filters_ref, hk, wide, slot, par_lane, k):
    eye = one_hot((k, k), lambda i, j: i == j)
    both = jnp.concatenate([dot_nt(eye, filters_ref[c]).astype(BF) for c in range(2)], axis=0)
    for b in range(slot):
        parent = parent_ref[b]
        held = jnp.maximum(parent, 0)
        lowered = dot_nn(both, group_all[held // par_lane, held % par_lane] if par_lane > 1 else group_all[held, 0])
        code = child_ref[b]
        upper = code >= 4
        corner = jnp.where(upper, code - 4, code)
        corner = jnp.where(parent >= 0, corner, -1)
        chosen = jnp.where(upper, lowered[k:], lowered[:k])
        for c in range(4):
            wide[c, b * k : (b + 1) * k, :] = jnp.where(corner == c, chosen, 0.0).astype(BF)
    total = dot_nn(wide[0], hk[0])
    for c in range(1, 4):
        total = total + dot_nn(wide[c], hk[c])
    return total


def body(
    fine_in,
    counts,
    neighbour_refs,
    offset_codes,
    neighbour_mask,
    send_slots,
    parent_of,
    child_code,
    coarse_refs,
    coarse_codes,
    coarse_mask,
    ops_x,
    ops_y,
    ops_z,
    filters,
):
    n_grp, n_lane = lax.axis_size("grp"), lax.axis_size("lane")
    n_dev = n_grp * n_lane
    k = filters.shape[1]
    kk = k * k
    slot = fine_in.shape[1]
    cap = send_slots.shape[2] // n_dev
    par_lane = coarse_refs.shape[0]
    terms = ops_x.shape[1]
    dims = (n_grp, n_lane, cap, slot, par_lane, k, terms)
    pool_size = slot + n_dev * cap + 1
    int32 = jnp.int32
    vmem = pl.BlockSpec(memory_space=pltpu.VMEM)
    hbm = pl.BlockSpec(memory_space=pl.ANY)
    dma = pltpu.SemaphoreType.DMA
    return pl.pallas_call(
        functools.partial(tree_kernel, dims),
        out_shape=(
            jax.ShapeDtypeStruct(fine_in.shape, BF),
            jax.ShapeDtypeStruct((par_lane, k, kk), BF),
        ),
        in_specs=[hbm] * 15,
        out_specs=(vmem, vmem),
        scratch_shapes=[
            pltpu.SMEM((2,), int32),
            pltpu.VMEM(neighbour_refs.shape, int32),
            pltpu.VMEM(offset_codes.shape, int32),
            pltpu.VMEM(neighbour_mask.shape, int32),
            pltpu.SMEM(send_slots.shape, int32),
            pltpu.SMEM(parent_of.shape, int32),
            pltpu.SMEM(child_code.shape, int32),
            pltpu.VMEM(coarse_refs.shape, int32),
            pltpu.VMEM(coarse_codes.shape, int32),
            pltpu.VMEM(coarse_mask.shape, int32),
            pltpu.VMEM(ops_x.shape, BF),
            pltpu.VMEM(ops_y.shape, BF),
            pltpu.VMEM(ops_z.shape, BF),
            pltpu.VMEM(filters.shape, BF),
            pltpu.VMEM((2, slot, 128), int32),
            pltpu.VMEM((par_lane, 128), int32),
            pltpu.SMEM((2, slot, 128), int32),
            pltpu.SMEM((par_lane, 128), int32),
            pltpu.VMEM((slot, k, kk), BF),
            pltpu.VMEM((slot, k, kk), BF),
            pltpu.VMEM((pool_size, k, kk), BF),
            pltpu.VMEM((pool_size, k, kk), BF),
            pltpu.VMEM((2, n_dev, cap, k, kk), BF),
            pltpu.VMEM((n_lane, par_lane, k, kk), F32),
            pltpu.VMEM((n_lane, par_lane, k, kk), F32),
            pltpu.VMEM((n_dev * par_lane + 1, k, kk), BF),
            pltpu.VMEM((n_lane, par_lane, k, kk), BF),
            pltpu.VMEM((4, kk, kk), BF),
            pltpu.VMEM((3, terms, PLANES * kk, kk), BF),
            pltpu.VMEM((terms, slot * k, PLANES * kk), BF),
            pltpu.VMEM((4, slot * k, kk), BF),
            dma((16,)),
            dma,
            dma,
            dma,
            dma,
            dma,
            dma,
            dma,
            dma,
            dma((2,)),
            dma((2,)),
        ],
        compiler_params=pltpu.CompilerParams(
            collective_id=0, has_side_effects=True, vmem_limit_bytes=56 * 1024 * 1024
        ),
    )(
        fine_in,
        counts.reshape(-1),
        neighbour_refs,
        offset_codes,
        neighbour_mask,
        send_slots,
        parent_of,
        child_code,
        coarse_refs,
        coarse_codes,
        coarse_mask,
        ops_x,
        ops_y,
        ops_z,
        filters,
    )


def solution(mesh):
    both = ("grp", "lane")
    in_specs = (
        P(None, both, None, None),
        P(None, both),
        P(None, both, None),
        P(None, both, None),
        P(None, both, None),
        P(None, both, None),
        P(both),
        P(both),
        P(both, None),
        P(both, None),
        P(both, None),
        P(),
        P(),
        P(),
        P(),
    )
    out_specs = (P(None, both, None, None), P(both, None, None))
    return jax.shard_map(body, mesh=mesh, in_specs=in_specs, out_specs=out_specs, check_vma=False)
```

```python
import functools

import jax
import jax.numpy as jnp
from jax import lax
from jax.experimental import pallas as pl
from jax.experimental.pallas import tpu as pltpu
from jax.sharding import PartitionSpec as P

MESH = pl.DeviceIdType.MESH
BF = jnp.bfloat16
F32 = jnp.float32
OFFSETS = 27
PLANES = 9
GROUP = 4


def dot_nn(a, b):
    return jnp.dot(a, b, preferred_element_type=F32)


def dot_nt(a, b):
    return lax.dot_general(a, b, (((1,), (1,)), ((), ())), preferred_element_type=F32)


def one_hot(shape, fn):
    rows = lax.broadcasted_iota(jnp.int32, shape, 0)
    cols = lax.broadcasted_iota(jnp.int32, shape, 1)
    return jnp.where(fn(rows, cols), 1.0, 0.0).astype(BF)


def spread_first(k):
    return one_hot((k, k * k), lambda i, j: (j >= i * k) & (j < i * k + k))


def spread_second(k):
    return one_hot((k, k * k), lambda i, j: lax.rem(j, k) == i)


def kron_rows(left, right, k):
    return jnp.concatenate([(left[p : p + 1, :] * right).astype(BF) for p in range(k)], axis=0)


def build_filters(filters_ref, hk_ref, k):
    first, second = spread_first(k), spread_second(k)
    left = [dot_nn(filters_ref[c], first) for c in range(2)]
    right = [dot_nn(filters_ref[c], second) for c in range(2)]
    for cy in range(2):
        for cz in range(2):
            hk_ref[2 * cy + cz] = kron_rows(left[cy], right[cz], k)


def build_tables(level, ops_y_ref, ops_z_ref, kr_ref, k, terms):
    first, second = spread_first(k), spread_second(k)
    eye = one_hot((k, k), lambda i, j: i == j)
    kk = k * k

    def turned(matrix):
        return dot_nt(eye, matrix).astype(BF)

    def one_term(m, carry):
        right = [dot_nn(turned(ops_z_ref[level, m, c]), second) for c in range(3)]
        for cy in range(3):
            left = dot_nn(turned(ops_y_ref[level, m, cy]), first)
            for cz in range(3):
                at = (3 * cy + cz) * kk
                kr_ref[m, at : at + kk, :] = kron_rows(left, right[cz], k)
        return carry

    lax.fori_loop(0, terms, one_term, 0)


def build_rows(level, ops_x_ref, group, k, terms):
    width = group * 3 * k
    blocks = []
    stacked = [
        jnp.concatenate([ops_x_ref[level, m, c] for m in range(terms)], axis=0) for c in range(3)
    ]
    for g in range(group):
        total = None
        for c in range(3):
            offset = (g * 3 + c) * k
            part = dot_nn(stacked[c], one_hot((k, width), lambda i, j: j == i + offset))
            total = part if total is None else total + part
        blocks.append(total.astype(BF))
    return jnp.concatenate(
        [blocks[g][m * k : (m + 1) * k] for m in range(terms) for g in range(group)], axis=0
    )


def spread_group(base, group, rows_mat, load, s_ref, k, terms):
    for plane in range(PLANES):
        source = jnp.concatenate(
            [load(base + g, 9 * c + plane) for g in range(group) for c in range(3)], axis=0
        )
        out = dot_nn(rows_mat, source).astype(BF)
        span = group * k
        for m in range(terms):
            s_ref[m, pl.ds(base * k, span), plane * k * k : (plane + 1) * k * k] = out[
                m * span : (m + 1) * span
            ]


def apply_tables(s_ref, kr_ref, rows, k, terms):
    def one_term(m, total):
        return total + dot_nn(s_ref[m, pl.ds(0, rows), :], kr_ref[m])

    return lax.fori_loop(0, terms, one_term, jnp.zeros((rows, k * k), F32))


def fill_index(refs, codes, mask, empty, out_ref, at):
    rows, slots = refs.shape
    code_of = lax.broadcasted_iota(jnp.int32, (rows, 128), 1)
    total = jnp.full((rows, 128), empty, jnp.int32)
    for j in range(slots):
        hit = (codes[:, j : j + 1] == code_of) & (mask[:, j : j + 1] == 1)
        total = jnp.where(hit, refs[:, j : j + 1], total)
    out_ref[at] = total


def tree_kernel(
    dims,
    fine_hbm,
    counts_hbm,
    refs_hbm,
    codes_hbm,
    mask_hbm,
    slots_hbm,
    parent_hbm,
    child_hbm,
    crefs_hbm,
    ccodes_hbm,
    cmask_hbm,
    ops_x_hbm,
    ops_y_hbm,
    ops_z_hbm,
    filters_hbm,
    out_ref,
    coarse_out,
    counts_ref,
    refs_ref,
    codes_ref,
    mask_ref,
    slots_ref,
    parent_ref,
    child_ref,
    crefs_ref,
    ccodes_ref,
    cmask_ref,
    ops_x_ref,
    ops_y_ref,
    ops_z_ref,
    filters_ref,
    idx_vec,
    cidx_vec,
    idx_ref,
    cidx_ref,
    own_0,
    own_1,
    pool_0,
    pool_1,
    packed_own,
    packed_mate,
    mate_0,
    mate_1,
    slots_vec,
    mate_slots,
    partial,
    rs_buf,
    coarse_all,
    group_all,
    hk,
    kr,
    s_buf,
    wide,
    in_sems,
    send_rs,
    recv_rs,
    send_ag,
    recv_ag,
    send_pass,
    recv_pass,
    send_co,
    recv_co,
    send_fine_sem,
    recv_fine,
    send_mate_sem,
    recv_mate,
):
    n_grp, n_lane, cap, slot, par_lane, k, terms = dims
    n_dev = n_grp * n_lane
    own, pool = (own_0, own_1), (pool_0, pool_1)
    mate_blocks = (mate_0, mate_1)
    grp = lax.axis_index("grp")
    lane = lax.axis_index("lane")
    me = grp * n_lane + lane

    def coords(d):
        return (lax.div(d, n_lane), lax.rem(d, n_lane))

    barrier = pltpu.get_barrier_semaphore()

    def greet(i, carry):
        pl.semaphore_signal(
            barrier, inc=1, device_id=coords(lax.rem(me + i, n_dev)), device_id_type=MESH
        )
        return carry

    fetches = [
        pltpu.make_async_copy(src, dst, in_sems.at[i])
        for i, (src, dst) in enumerate(
            [
                (slots_hbm, slots_ref),
                (fine_hbm.at[0], own_0),
                (filters_hbm, filters_ref),
                (fine_hbm.at[1], own_1),
                (child_hbm, child_ref),
                (parent_hbm, parent_ref),
                (crefs_hbm, crefs_ref),
                (ccodes_hbm, ccodes_ref),
                (cmask_hbm, cmask_ref),
                (ops_x_hbm, ops_x_ref),
                (ops_y_hbm, ops_y_ref),
                (ops_z_hbm, ops_z_ref),
                (refs_hbm, refs_ref),
                (codes_hbm, codes_ref),
                (mask_hbm, mask_ref),
                (counts_hbm, counts_ref),
            ]
        )
    ]
    for fetch in fetches:
        fetch.start()
    lax.fori_loop(1, n_dev, greet, 0)

    half = n_dev // 2
    lane_half = n_lane // 2
    side = lax.div(lane, lane_half)
    mate_lane = lax.rem(lane + lane_half, n_lane)
    mate = grp * n_lane + mate_lane
    place = grp * lane_half + lane - side * lane_half

    def peer(h):
        return lax.div(h, lane_half), side * lane_half + lax.rem(h, lane_half)

    def send_mate(src, dst, at):
        pltpu.make_async_remote_copy(
            src_ref=src,
            dst_ref=dst,
            send_sem=send_mate_sem.at[at],
            recv_sem=recv_mate.at[at],
            device_id=(grp, mate_lane),
            device_id_type=MESH,
        ).start()

    def send_fine(level, owner, blocks, slots, packed):
        def one(i, carry):
            h = lax.rem(place + i, half)
            to_grp, to_lane = peer(h)
            d = to_grp * n_lane + to_lane
            for c in range(cap):
                packed[level, h, c] = blocks[slots[level, 0, d * cap + c]]

            @pl.when(i > 0)
            def _():
                pltpu.make_async_remote_copy(
                    src_ref=packed.at[level, h],
                    dst_ref=pool[level].at[pl.ds(slot + owner * cap, cap)],
                    send_sem=send_fine_sem.at[level],
                    recv_sem=recv_fine.at[level],
                    device_id=(to_grp, to_lane),
                    device_id_type=MESH,
                ).start()

            return carry

        lax.fori_loop(0, half, one, 0)
        pool[level][pl.ds(slot + owner * cap, cap)] = packed[level, place]

    def pass_mate(level):
        await_bytes(mate_blocks[level], recv_mate.at[level])
        send_fine(level, mate, mate_blocks[level], mate_slots, packed_mate)

    def await_bytes(ref, sem):
        pltpu.make_async_copy(ref, ref, sem).wait()

    def keep_own(level):
        pool[level][slot + n_dev * cap] = jnp.zeros((k, k * k), BF)
        pool[level][pl.ds(0, slot)] = own[level][...]

    pl.semaphore_wait(barrier, n_dev - 1)
    send_mate(slots_hbm, slots_vec, 2)
    send_mate(fine_hbm.at[0], mate_0, 0)
    send_mate(fine_hbm.at[1], mate_1, 1)
    for fetch in fetches[:2]:
        fetch.wait()
    send_fine(0, me, own_0, slots_ref, packed_own)

    for fetch in fetches[2:6]:
        fetch.wait()
    build_filters(filters_ref, hk, k)
    both = jnp.concatenate([filters_ref[0], filters_ref[1]], axis=0)
    for b in range(slot):
        lifted = dot_nn(both, own_1[b])
        code = child_ref[b]
        upper = code >= 4
        corner = jnp.where(upper, code - 4, code)
        chosen = jnp.where(upper, lifted[k:], lifted[:k])
        for c in range(4):
            wide[c, b * k : (b + 1) * k, :] = jnp.where(corner == c, chosen, 0.0).astype(BF)
    terms_up = dot_nt(wide[0], hk[0])
    for c in range(1, 4):
        terms_up = terms_up + dot_nt(wide[c], hk[c])
    for t in range(n_lane * par_lane):
        total = jnp.zeros((k, k * k), F32)
        for b in range(slot):
            total = total + jnp.where(parent_ref[b] == t, terms_up[b * k : (b + 1) * k], 0.0)
        partial[t // par_lane, t % par_lane] = total

    def send_partial(i, carry):
        to = lax.rem(lane + i, n_lane)
        pltpu.make_async_remote_copy(
            src_ref=partial.at[to],
            dst_ref=rs_buf.at[lane],
            send_sem=send_rs,
            recv_sem=recv_rs,
            device_id=(grp, to),
            device_id_type=MESH,
        ).start()
        return carry

    lax.fori_loop(1, n_lane, send_partial, 0)
    await_bytes(slots_vec, recv_mate.at[2])
    slots_copy = pltpu.make_async_copy(slots_vec, mate_slots, in_sems.at[2])
    slots_copy.start()
    slots_copy.wait()
    pass_mate(0)
    send_fine(1, me, own_1, slots_ref, packed_own)

    rs_buf[lane] = partial[lane]
    coarse_all[n_dev * par_lane] = jnp.zeros((k, k * k), BF)
    keep_own(0)
    keep_own(1)
    for fetch in fetches[6:]:
        fetch.wait()
    fill_index(crefs_ref[...], ccodes_ref[...], cmask_ref[...], n_dev * par_lane, cidx_vec, ...)
    for level in range(2):
        fill_index(
            refs_ref[level], codes_ref[level], mask_ref[level], slot + n_dev * cap, idx_vec, level
        )
    table_copies = [
        pltpu.make_async_copy(cidx_vec, cidx_ref, in_sems.at[0]),
        pltpu.make_async_copy(idx_vec, idx_ref, in_sems.at[1]),
    ]
    for copy in table_copies:
        copy.start()
    build_tables(0, ops_y_ref, ops_z_ref, kr.at[0], k, terms)

    await_bytes(rs_buf.at[pl.ds(0, n_lane - 1)], recv_rs)
    total = rs_buf[0]
    for t in range(1, n_lane):
        total = total + rs_buf[t]
    coarse_all[pl.ds(me * par_lane, par_lane)] = total.astype(BF)

    odd = lax.rem(grp, 2)
    twin = grp + 1 - 2 * odd

    def send_coarse(i, carry):
        at = lax.rem(lax.div(grp, 2) * n_lane + lane + i, half)
        mine = coarse_all.at[pl.ds(me * par_lane, par_lane)]
        pltpu.make_async_remote_copy(
            src_ref=mine,
            dst_ref=mine,
            send_sem=send_ag,
            recv_sem=recv_ag,
            device_id=(2 * lax.div(at, n_lane) + odd, lax.rem(at, n_lane)),
            device_id_type=MESH,
        ).start()
        return carry

    lax.fori_loop(1, half, send_coarse, 0)
    pass_mate(1)
    for level in (2, 1):
        build_tables(level, ops_y_ref, ops_z_ref, kr.at[level], k, terms)
    for copy in table_copies:
        copy.wait()

    await_bytes(pool_0.at[pl.ds(0, (n_dev - 2) * cap)], recv_fine.at[0])
    result = fine_operator(0, pool_0, idx_ref, ops_x_ref, kr.at[0], s_buf, slot, k, terms)
    for b in range(slot):
        value = jnp.where(b < counts_ref[0], result[b * k : (b + 1) * k], 0.0)
        out_ref[0, b] = value.astype(BF)

    await_bytes(coarse_all.at[pl.ds(0, (half - 1) * par_lane)], recv_ag)
    for pair in range(n_grp // 2):
        held = coarse_all.at[pl.ds((2 * pair + odd) * n_lane * par_lane, n_lane * par_lane)]
        pltpu.make_async_remote_copy(
            src_ref=held,
            dst_ref=held,
            send_sem=send_pass,
            recv_sem=recv_pass,
            device_id=(twin, lane),
            device_id_type=MESH,
        ).start()
    rows_mat = build_rows(2, ops_x_ref, 1, k, terms)
    await_bytes(coarse_all.at[pl.ds(0, half * par_lane)], recv_pass)
    for b in range(par_lane):
        spread_group(
            b, 1, rows_mat, lambda i, code: coarse_all[cidx_ref[i, code]], s_buf, k, terms
        )
    result = apply_tables(s_buf, kr.at[2], par_lane * k, k, terms).astype(BF)
    for b in range(par_lane):
        group_all[lane, b] = result[b * k : (b + 1) * k]
        coarse_out[b] = result[b * k : (b + 1) * k]

    def send_result(i, carry):
        to = lax.rem(lane + i, n_lane)
        pltpu.make_async_remote_copy(
            src_ref=group_all.at[lane],
            dst_ref=group_all.at[lane],
            send_sem=send_co,
            recv_sem=recv_co,
            device_id=(grp, to),
            device_id_type=MESH,
        ).start()
        return carry

    lax.fori_loop(1, n_lane, send_result, 0)

    await_bytes(pool_1.at[pl.ds(0, (n_dev - 2) * cap)], recv_fine.at[1])
    result = fine_operator(1, pool_1, idx_ref, ops_x_ref, kr.at[1], s_buf, slot, k, terms)
    await_bytes(group_all.at[pl.ds(0, n_lane - 1)], recv_co)
    correction = drop(
        group_all, parent_ref, child_ref, filters_ref, hk, wide, slot, par_lane, k
    )
    for b in range(slot):
        value = jnp.where(b < counts_ref[1], result[b * k : (b + 1) * k], 0.0)
        out_ref[1, b] = (value + correction[b * k : (b + 1) * k]).astype(BF)

    await_bytes(rs_buf.at[pl.ds(0, n_lane - 1)], send_rs)
    await_bytes(coarse_all.at[pl.ds(0, (half - 1) * par_lane)], send_ag)
    await_bytes(coarse_all.at[pl.ds(0, half * par_lane)], send_pass)
    await_bytes(group_all.at[pl.ds(0, n_lane - 1)], send_co)
    for level in range(2):
        await_bytes(pool[level].at[pl.ds(0, (n_dev - 2) * cap)], send_fine_sem.at[level])
        await_bytes(mate_blocks[level], send_mate_sem.at[level])
    await_bytes(slots_vec, send_mate_sem.at[2])


def fine_operator(level, pool, idx_ref, ops_x_ref, kr, s_buf, slot, k, terms):
    group = GROUP if slot % GROUP == 0 else 1
    rows_mat = build_rows(level, ops_x_ref, group, k, terms)

    def one_group(g, carry):
        spread_group(
            pl.multiple_of(g * group, group),
            group,
            rows_mat,
            lambda i, code: pool[idx_ref[level, i, code]],
            s_buf,
            k,
            terms,
        )
        return carry

    lax.fori_loop(0, slot // group, one_group, 0)
    return apply_tables(s_buf, kr, slot * k, k, terms)


def drop(group_all, parent_ref, child_ref, filters_ref, hk, wide, slot, par_lane, k):
    eye = one_hot((k, k), lambda i, j: i == j)
    both = jnp.concatenate([dot_nt(eye, filters_ref[c]).astype(BF) for c in range(2)], axis=0)
    for b in range(slot):
        parent = parent_ref[b]
        held = jnp.maximum(parent, 0)
        lowered = dot_nn(both, group_all[held // par_lane, held % par_lane] if par_lane > 1 else group_all[held, 0])
        code = child_ref[b]
        upper = code >= 4
        corner = jnp.where(upper, code - 4, code)
        corner = jnp.where(parent >= 0, corner, -1)
        chosen = jnp.where(upper, lowered[k:], lowered[:k])
        for c in range(4):
            wide[c, b * k : (b + 1) * k, :] = jnp.where(corner == c, chosen, 0.0).astype(BF)
    total = dot_nn(wide[0], hk[0])
    for c in range(1, 4):
        total = total + dot_nn(wide[c], hk[c])
    return total


def body(
    fine_in,
    counts,
    neighbour_refs,
    offset_codes,
    neighbour_mask,
    send_slots,
    parent_of,
    child_code,
    coarse_refs,
    coarse_codes,
    coarse_mask,
    ops_x,
    ops_y,
    ops_z,
    filters,
):
    n_grp, n_lane = lax.axis_size("grp"), lax.axis_size("lane")
    n_dev = n_grp * n_lane
    k = filters.shape[1]
    kk = k * k
    slot = fine_in.shape[1]
    cap = send_slots.shape[2] // n_dev
    par_lane = coarse_refs.shape[0]
    terms = ops_x.shape[1]
    dims = (n_grp, n_lane, cap, slot, par_lane, k, terms)
    pool_size = slot + n_dev * cap + 1
    int32 = jnp.int32
    vmem = pl.BlockSpec(memory_space=pltpu.VMEM)
    hbm = pl.BlockSpec(memory_space=pl.ANY)
    dma = pltpu.SemaphoreType.DMA
    return pl.pallas_call(
        functools.partial(tree_kernel, dims),
        out_shape=(
            jax.ShapeDtypeStruct(fine_in.shape, BF),
            jax.ShapeDtypeStruct((par_lane, k, kk), BF),
        ),
        in_specs=[hbm] * 15,
        out_specs=(vmem, vmem),
        scratch_shapes=[
            pltpu.SMEM((2,), int32),
            pltpu.VMEM(neighbour_refs.shape, int32),
            pltpu.VMEM(offset_codes.shape, int32),
            pltpu.VMEM(neighbour_mask.shape, int32),
            pltpu.SMEM(send_slots.shape, int32),
            pltpu.SMEM(parent_of.shape, int32),
            pltpu.SMEM(child_code.shape, int32),
            pltpu.VMEM(coarse_refs.shape, int32),
            pltpu.VMEM(coarse_codes.shape, int32),
            pltpu.VMEM(coarse_mask.shape, int32),
            pltpu.VMEM(ops_x.shape, BF),
            pltpu.VMEM(ops_y.shape, BF),
            pltpu.VMEM(ops_z.shape, BF),
            pltpu.VMEM(filters.shape, BF),
            pltpu.VMEM((2, slot, 128), int32),
            pltpu.VMEM((par_lane, 128), int32),
            pltpu.SMEM((2, slot, 128), int32),
            pltpu.SMEM((par_lane, 128), int32),
            pltpu.VMEM((slot, k, kk), BF),
            pltpu.VMEM((slot, k, kk), BF),
            pltpu.VMEM((pool_size, k, kk), BF),
            pltpu.VMEM((pool_size, k, kk), BF),
            pltpu.VMEM((2, n_dev // 2, cap, k, kk), BF),
            pltpu.VMEM((2, n_dev // 2, cap, k, kk), BF),
            pltpu.VMEM((slot, k, kk), BF),
            pltpu.VMEM((slot, k, kk), BF),
            pltpu.VMEM(send_slots.shape, int32),
            pltpu.SMEM(send_slots.shape, int32),
            pltpu.VMEM((n_lane, par_lane, k, kk), F32),
            pltpu.VMEM((n_lane, par_lane, k, kk), F32),
            pltpu.VMEM((n_dev * par_lane + 1, k, kk), BF),
            pltpu.VMEM((n_lane, par_lane, k, kk), BF),
            pltpu.VMEM((4, kk, kk), BF),
            pltpu.VMEM((3, terms, PLANES * kk, kk), BF),
            pltpu.VMEM((terms, slot * k, PLANES * kk), BF),
            pltpu.VMEM((4, slot * k, kk), BF),
            dma((16,)),
            dma,
            dma,
            dma,
            dma,
            dma,
            dma,
            dma,
            dma,
            dma((2,)),
            dma((2,)),
            dma((3,)),
            dma((3,)),
        ],
        compiler_params=pltpu.CompilerParams(
            collective_id=0, has_side_effects=True, vmem_limit_bytes=56 * 1024 * 1024
        ),
    )(
        fine_in,
        counts.reshape(-1),
        neighbour_refs,
        offset_codes,
        neighbour_mask,
        send_slots,
        parent_of,
        child_code,
        coarse_refs,
        coarse_codes,
        coarse_mask,
        ops_x,
        ops_y,
        ops_z,
        filters,
    )


def solution(mesh):
    both = ("grp", "lane")
    in_specs = (
        P(None, both, None, None),
        P(None, both),
        P(None, both, None),
        P(None, both, None),
        P(None, both, None),
        P(None, both, None),
        P(both),
        P(both),
        P(both, None),
        P(both, None),
        P(both, None),
        P(),
        P(),
        P(),
        P(),
    )
    out_specs = (P(None, both, None, None), P(both, None, None))
    return jax.shard_map(body, mesh=mesh, in_specs=in_specs, out_specs=out_specs, check_vma=False)
```

```python
import functools

import jax
import jax.numpy as jnp
from jax import lax
from jax.experimental import pallas as pl
from jax.experimental.pallas import tpu as pltpu
from jax.sharding import PartitionSpec as P

MESH = pl.DeviceIdType.MESH
BF = jnp.bfloat16
F32 = jnp.float32
OFFSETS = 27
PLANES = 9
GROUP = 4


def dot_nn(a, b):
    return jnp.dot(a, b, preferred_element_type=F32)


def dot_nt(a, b):
    return lax.dot_general(a, b, (((1,), (1,)), ((), ())), preferred_element_type=F32)


def one_hot(shape, fn):
    rows = lax.broadcasted_iota(jnp.int32, shape, 0)
    cols = lax.broadcasted_iota(jnp.int32, shape, 1)
    return jnp.where(fn(rows, cols), 1.0, 0.0).astype(BF)


def spread_first(k):
    return one_hot((k, k * k), lambda i, j: (j >= i * k) & (j < i * k + k))


def spread_second(k):
    return one_hot((k, k * k), lambda i, j: lax.rem(j, k) == i)


def row_copies(left, k):
    return [jnp.broadcast_to(left[p : p + 1, :], left.shape).astype(BF) for p in range(k)]


def kron_store(out_ref, rows, right, k):
    for p in range(k):
        out_ref[p * k : (p + 1) * k, :] = rows[p] * right


def build_filters(filters_ref, hk_ref, k):
    first, second = spread_first(k), spread_second(k)
    right = [dot_nn(filters_ref[c], second).astype(BF) for c in range(2)]
    for cy in range(2):
        rows = row_copies(dot_nn(filters_ref[cy], first), k)
        for cz in range(2):
            kron_store(hk_ref.at[2 * cy + cz], rows, right[cz], k)


def build_tables(level, ops_y_ref, ops_z_ref, kr_ref, k, terms):
    first, second = spread_first(k), spread_second(k)
    eye = one_hot((k, k), lambda i, j: i == j)
    kk = k * k

    def turned(matrix):
        return dot_nt(eye, matrix).astype(BF)

    def one_term(m, carry):
        right = [dot_nn(turned(ops_z_ref[level, m, c]), second).astype(BF) for c in range(3)]
        for cy in range(3):
            rows = row_copies(dot_nn(turned(ops_y_ref[level, m, cy]), first), k)
            for cz in range(3):
                at = (3 * cy + cz) * kk
                kron_store(kr_ref.at[m, pl.ds(at, kk)], rows, right[cz], k)
        return carry

    lax.fori_loop(0, terms, one_term, 0)


def build_rows(level, ops_x_ref, group, k, terms):
    width = group * 3 * k
    blocks = []
    stacked = [
        jnp.concatenate([ops_x_ref[level, m, c] for m in range(terms)], axis=0) for c in range(3)
    ]
    for g in range(group):
        total = None
        for c in range(3):
            offset = (g * 3 + c) * k
            part = dot_nn(stacked[c], one_hot((k, width), lambda i, j: j == i + offset))
            total = part if total is None else total + part
        blocks.append(total.astype(BF))
    return jnp.concatenate(
        [blocks[g][m * k : (m + 1) * k] for m in range(terms) for g in range(group)], axis=0
    )


def spread_group(base, group, rows_mat, load, s_ref, k, terms):
    for plane in range(PLANES):
        source = jnp.concatenate(
            [load(base + g, 9 * c + plane) for g in range(group) for c in range(3)], axis=0
        )
        out = dot_nn(rows_mat, source).astype(BF)
        span = group * k
        for m in range(terms):
            s_ref[m, pl.ds(base * k, span), plane * k * k : (plane + 1) * k * k] = out[
                m * span : (m + 1) * span
            ]


def apply_tables(s_ref, kr_ref, rows, k, terms):
    def one_term(m, total):
        return total + dot_nn(s_ref[m, pl.ds(0, rows), :], kr_ref[m])

    return lax.fori_loop(0, terms, one_term, jnp.zeros((rows, k * k), F32))


def fill_index(refs, codes, mask, empty, out_ref, at):
    rows, slots = refs.shape
    code_of = lax.broadcasted_iota(jnp.int32, (rows, 128), 1)
    total = jnp.full((rows, 128), empty, jnp.int32)
    for j in range(slots):
        hit = (codes[:, j : j + 1] == code_of) & (mask[:, j : j + 1] == 1)
        total = jnp.where(hit, refs[:, j : j + 1], total)
    out_ref[at] = total


def tree_kernel(
    dims,
    fine_hbm,
    counts_hbm,
    refs_hbm,
    codes_hbm,
    mask_hbm,
    slots_hbm,
    parent_hbm,
    child_hbm,
    crefs_hbm,
    ccodes_hbm,
    cmask_hbm,
    ops_x_hbm,
    ops_y_hbm,
    ops_z_hbm,
    filters_hbm,
    out_ref,
    coarse_out,
    counts_ref,
    refs_ref,
    codes_ref,
    mask_ref,
    slots_ref,
    parent_ref,
    child_ref,
    crefs_ref,
    ccodes_ref,
    cmask_ref,
    ops_x_ref,
    ops_y_ref,
    ops_z_ref,
    filters_ref,
    idx_vec,
    cidx_vec,
    idx_ref,
    cidx_ref,
    own_0,
    own_1,
    pool_0,
    pool_1,
    packed_own,
    packed_mate,
    mate_0,
    mate_1,
    slots_vec,
    mate_slots,
    partial,
    rs_buf,
    coarse_all,
    group_all,
    hk,
    kr,
    s_buf,
    wide,
    in_sems,
    send_rs,
    recv_rs,
    send_ag,
    recv_ag,
    send_pass,
    recv_pass,
    send_co,
    recv_co,
    send_fine_sem,
    recv_fine,
    send_mate_sem,
    recv_mate,
):
    n_grp, n_lane, cap, slot, par_lane, k, terms = dims
    n_dev = n_grp * n_lane
    own, pool = (own_0, own_1), (pool_0, pool_1)
    mate_blocks = (mate_0, mate_1)
    grp = lax.axis_index("grp")
    lane = lax.axis_index("lane")
    me = grp * n_lane + lane

    def coords(d):
        return (lax.div(d, n_lane), lax.rem(d, n_lane))

    barrier = pltpu.get_barrier_semaphore()

    def greet(i, carry):
        pl.semaphore_signal(
            barrier, inc=1, device_id=coords(lax.rem(me + i, n_dev)), device_id_type=MESH
        )
        return carry

    fetches = [
        pltpu.make_async_copy(src, dst, in_sems.at[i])
        for i, (src, dst) in enumerate(
            [
                (ops_y_hbm, ops_y_ref),
                (ops_z_hbm, ops_z_ref),
                (slots_hbm, slots_ref),
                (fine_hbm.at[0], own_0),
                (filters_hbm, filters_ref),
                (fine_hbm.at[1], own_1),
                (child_hbm, child_ref),
                (parent_hbm, parent_ref),
                (crefs_hbm, crefs_ref),
                (ccodes_hbm, ccodes_ref),
                (cmask_hbm, cmask_ref),
                (ops_x_hbm, ops_x_ref),
                (refs_hbm, refs_ref),
                (codes_hbm, codes_ref),
                (mask_hbm, mask_ref),
                (counts_hbm, counts_ref),
            ]
        )
    ]
    for fetch in fetches:
        fetch.start()
    lax.fori_loop(1, n_dev, greet, 0)

    half = n_dev // 2
    lane_half = n_lane // 2
    side = lax.div(lane, lane_half)
    mate_lane = lax.rem(lane + lane_half, n_lane)
    mate = grp * n_lane + mate_lane
    place = grp * lane_half + lane - side * lane_half

    def peer(h):
        return lax.div(h, lane_half), side * lane_half + lax.rem(h, lane_half)

    def send_mate(src, dst, at):
        pltpu.make_async_remote_copy(
            src_ref=src,
            dst_ref=dst,
            send_sem=send_mate_sem.at[at],
            recv_sem=recv_mate.at[at],
            device_id=(grp, mate_lane),
            device_id_type=MESH,
        ).start()

    def send_fine(level, owner, blocks, slots, packed):
        def one(i, carry):
            h = lax.rem(place + i, half)
            to_grp, to_lane = peer(h)
            d = to_grp * n_lane + to_lane
            for c in range(cap):
                packed[level, h, c] = blocks[slots[level, 0, d * cap + c]]

            @pl.when(i > 0)
            def _():
                pltpu.make_async_remote_copy(
                    src_ref=packed.at[level, h],
                    dst_ref=pool[level].at[pl.ds(slot + owner * cap, cap)],
                    send_sem=send_fine_sem.at[level],
                    recv_sem=recv_fine.at[level],
                    device_id=(to_grp, to_lane),
                    device_id_type=MESH,
                ).start()

            return carry

        lax.fori_loop(0, half, one, 0)
        pool[level][pl.ds(slot + owner * cap, cap)] = packed[level, place]

    def pass_mate(level):
        await_bytes(mate_blocks[level], recv_mate.at[level])
        send_fine(level, mate, mate_blocks[level], mate_slots, packed_mate)

    def await_bytes(ref, sem):
        pltpu.make_async_copy(ref, ref, sem).wait()

    def keep_own(level):
        pool[level][slot + n_dev * cap] = jnp.zeros((k, k * k), BF)
        pool[level][pl.ds(0, slot)] = own[level][...]

    for fetch in fetches[:2]:
        fetch.wait()
    build_tables(2, ops_y_ref, ops_z_ref, kr.at[2], k, terms)
    pl.semaphore_wait(barrier, n_dev - 1)
    send_mate(slots_hbm, slots_vec, 2)
    send_mate(fine_hbm.at[0], mate_0, 0)
    send_mate(fine_hbm.at[1], mate_1, 1)
    for fetch in fetches[2:4]:
        fetch.wait()
    send_fine(0, me, own_0, slots_ref, packed_own)

    for fetch in fetches[4:8]:
        fetch.wait()
    build_filters(filters_ref, hk, k)
    await_bytes(slots_vec, recv_mate.at[2])
    slots_copy = pltpu.make_async_copy(slots_vec, mate_slots, in_sems.at[2])
    slots_copy.start()
    both = jnp.concatenate([filters_ref[0], filters_ref[1]], axis=0)
    for b in range(slot):
        lifted = dot_nn(both, own_1[b])
        code = child_ref[b]
        upper = code >= 4
        corner = jnp.where(upper, code - 4, code)
        chosen = jnp.where(upper, lifted[k:], lifted[:k])
        for c in range(4):
            wide[c, b * k : (b + 1) * k, :] = jnp.where(corner == c, chosen, 0.0).astype(BF)
    terms_up = dot_nt(wide[0], hk[0])
    for c in range(1, 4):
        terms_up = terms_up + dot_nt(wide[c], hk[c])
    for t in range(n_lane * par_lane):
        total = jnp.zeros((k, k * k), F32)
        for b in range(slot):
            total = total + jnp.where(parent_ref[b] == t, terms_up[b * k : (b + 1) * k], 0.0)
        partial[t // par_lane, t % par_lane] = total

    def send_partial(i, carry):
        to = lax.rem(lane + i, n_lane)
        pltpu.make_async_remote_copy(
            src_ref=partial.at[to],
            dst_ref=rs_buf.at[lane],
            send_sem=send_rs,
            recv_sem=recv_rs,
            device_id=(grp, to),
            device_id_type=MESH,
        ).start()
        return carry

    lax.fori_loop(1, n_lane, send_partial, 0)
    slots_copy.wait()
    pass_mate(0)
    send_fine(1, me, own_1, slots_ref, packed_own)

    rs_buf[lane] = partial[lane]
    coarse_all[n_dev * par_lane] = jnp.zeros((k, k * k), BF)
    keep_own(0)
    keep_own(1)
    for fetch in fetches[8:]:
        fetch.wait()
    fill_index(crefs_ref[...], ccodes_ref[...], cmask_ref[...], n_dev * par_lane, cidx_vec, ...)
    for level in range(2):
        fill_index(
            refs_ref[level], codes_ref[level], mask_ref[level], slot + n_dev * cap, idx_vec, level
        )
    table_copies = [
        pltpu.make_async_copy(cidx_vec, cidx_ref, in_sems.at[0]),
        pltpu.make_async_copy(idx_vec, idx_ref, in_sems.at[1]),
    ]
    for copy in table_copies:
        copy.start()
    build_tables(0, ops_y_ref, ops_z_ref, kr.at[0], k, terms)

    await_bytes(rs_buf.at[pl.ds(0, n_lane - 1)], recv_rs)
    total = rs_buf[0]
    for t in range(1, n_lane):
        total = total + rs_buf[t]
    coarse_all[pl.ds(me * par_lane, par_lane)] = total.astype(BF)

    odd = lax.rem(grp, 2)
    twin = grp + 1 - 2 * odd

    def send_coarse(i, carry):
        at = lax.rem(lax.div(grp, 2) * n_lane + lane + i, half)
        mine = coarse_all.at[pl.ds(me * par_lane, par_lane)]
        pltpu.make_async_remote_copy(
            src_ref=mine,
            dst_ref=mine,
            send_sem=send_ag,
            recv_sem=recv_ag,
            device_id=(2 * lax.div(at, n_lane) + odd, lax.rem(at, n_lane)),
            device_id_type=MESH,
        ).start()
        return carry

    lax.fori_loop(1, half, send_coarse, 0)
    pass_mate(1)
    build_tables(1, ops_y_ref, ops_z_ref, kr.at[1], k, terms)
    for copy in table_copies:
        copy.wait()

    await_bytes(coarse_all.at[pl.ds(0, (half - 1) * par_lane)], recv_ag)
    for pair in range(n_grp // 2):
        held = coarse_all.at[pl.ds((2 * pair + odd) * n_lane * par_lane, n_lane * par_lane)]
        pltpu.make_async_remote_copy(
            src_ref=held,
            dst_ref=held,
            send_sem=send_pass,
            recv_sem=recv_pass,
            device_id=(twin, lane),
            device_id_type=MESH,
        ).start()

    await_bytes(pool_0.at[pl.ds(0, (n_dev - 2) * cap)], recv_fine.at[0])
    result = fine_operator(0, pool_0, idx_ref, ops_x_ref, kr.at[0], s_buf, slot, k, terms)
    for b in range(slot):
        value = jnp.where(b < counts_ref[0], result[b * k : (b + 1) * k], 0.0)
        out_ref[0, b] = value.astype(BF)

    rows_mat = build_rows(2, ops_x_ref, 1, k, terms)
    await_bytes(coarse_all.at[pl.ds(0, half * par_lane)], recv_pass)
    for b in range(par_lane):
        spread_group(
            b, 1, rows_mat, lambda i, code: coarse_all[cidx_ref[i, code]], s_buf, k, terms
        )
    result = apply_tables(s_buf, kr.at[2], par_lane * k, k, terms).astype(BF)
    for b in range(par_lane):
        group_all[lane, b] = result[b * k : (b + 1) * k]
        coarse_out[b] = result[b * k : (b + 1) * k]

    def send_result(i, carry):
        to = lax.rem(lane + i, n_lane)
        pltpu.make_async_remote_copy(
            src_ref=group_all.at[lane],
            dst_ref=group_all.at[lane],
            send_sem=send_co,
            recv_sem=recv_co,
            device_id=(grp, to),
            device_id_type=MESH,
        ).start()
        return carry

    lax.fori_loop(1, n_lane, send_result, 0)

    await_bytes(pool_1.at[pl.ds(0, (n_dev - 2) * cap)], recv_fine.at[1])
    result = fine_operator(1, pool_1, idx_ref, ops_x_ref, kr.at[1], s_buf, slot, k, terms)
    await_bytes(group_all.at[pl.ds(0, n_lane - 1)], recv_co)
    correction = drop(
        group_all, parent_ref, child_ref, filters_ref, hk, wide, slot, par_lane, k
    )
    for b in range(slot):
        value = jnp.where(b < counts_ref[1], result[b * k : (b + 1) * k], 0.0)
        out_ref[1, b] = (value + correction[b * k : (b + 1) * k]).astype(BF)

    await_bytes(rs_buf.at[pl.ds(0, n_lane - 1)], send_rs)
    await_bytes(coarse_all.at[pl.ds(0, (half - 1) * par_lane)], send_ag)
    await_bytes(coarse_all.at[pl.ds(0, half * par_lane)], send_pass)
    await_bytes(group_all.at[pl.ds(0, n_lane - 1)], send_co)
    for level in range(2):
        await_bytes(pool[level].at[pl.ds(0, (n_dev - 2) * cap)], send_fine_sem.at[level])
        await_bytes(mate_blocks[level], send_mate_sem.at[level])
    await_bytes(slots_vec, send_mate_sem.at[2])


def fine_operator(level, pool, idx_ref, ops_x_ref, kr, s_buf, slot, k, terms):
    group = GROUP if slot % GROUP == 0 else 1
    rows_mat = build_rows(level, ops_x_ref, group, k, terms)

    def one_group(g, carry):
        spread_group(
            pl.multiple_of(g * group, group),
            group,
            rows_mat,
            lambda i, code: pool[idx_ref[level, i, code]],
            s_buf,
            k,
            terms,
        )
        return carry

    lax.fori_loop(0, slot // group, one_group, 0)
    return apply_tables(s_buf, kr, slot * k, k, terms)


def drop(group_all, parent_ref, child_ref, filters_ref, hk, wide, slot, par_lane, k):
    eye = one_hot((k, k), lambda i, j: i == j)
    both = jnp.concatenate([dot_nt(eye, filters_ref[c]).astype(BF) for c in range(2)], axis=0)
    for b in range(slot):
        parent = parent_ref[b]
        held = jnp.maximum(parent, 0)
        lowered = dot_nn(both, group_all[held // par_lane, held % par_lane] if par_lane > 1 else group_all[held, 0])
        code = child_ref[b]
        upper = code >= 4
        corner = jnp.where(upper, code - 4, code)
        corner = jnp.where(parent >= 0, corner, -1)
        chosen = jnp.where(upper, lowered[k:], lowered[:k])
        for c in range(4):
            wide[c, b * k : (b + 1) * k, :] = jnp.where(corner == c, chosen, 0.0).astype(BF)
    total = dot_nn(wide[0], hk[0])
    for c in range(1, 4):
        total = total + dot_nn(wide[c], hk[c])
    return total


def body(
    fine_in,
    counts,
    neighbour_refs,
    offset_codes,
    neighbour_mask,
    send_slots,
    parent_of,
    child_code,
    coarse_refs,
    coarse_codes,
    coarse_mask,
    ops_x,
    ops_y,
    ops_z,
    filters,
):
    n_grp, n_lane = lax.axis_size("grp"), lax.axis_size("lane")
    n_dev = n_grp * n_lane
    k = filters.shape[1]
    kk = k * k
    slot = fine_in.shape[1]
    cap = send_slots.shape[2] // n_dev
    par_lane = coarse_refs.shape[0]
    terms = ops_x.shape[1]
    dims = (n_grp, n_lane, cap, slot, par_lane, k, terms)
    pool_size = slot + n_dev * cap + 1
    int32 = jnp.int32
    vmem = pl.BlockSpec(memory_space=pltpu.VMEM)
    hbm = pl.BlockSpec(memory_space=pl.ANY)
    dma = pltpu.SemaphoreType.DMA
    return pl.pallas_call(
        functools.partial(tree_kernel, dims),
        out_shape=(
            pltpu.VMEM(fine_in.shape, BF),
            pltpu.VMEM((par_lane, k, kk), BF),
        ),
        in_specs=[hbm] * 15,
        out_specs=(vmem, vmem),
        scratch_shapes=[
            pltpu.SMEM((2,), int32),
            pltpu.VMEM(neighbour_refs.shape, int32),
            pltpu.VMEM(offset_codes.shape, int32),
            pltpu.VMEM(neighbour_mask.shape, int32),
            pltpu.SMEM(send_slots.shape, int32),
            pltpu.SMEM(parent_of.shape, int32),
            pltpu.SMEM(child_code.shape, int32),
            pltpu.VMEM(coarse_refs.shape, int32),
            pltpu.VMEM(coarse_codes.shape, int32),
            pltpu.VMEM(coarse_mask.shape, int32),
            pltpu.VMEM(ops_x.shape, BF),
            pltpu.VMEM(ops_y.shape, BF),
            pltpu.VMEM(ops_z.shape, BF),
            pltpu.VMEM(filters.shape, BF),
            pltpu.VMEM((2, slot, 128), int32),
            pltpu.VMEM((par_lane, 128), int32),
            pltpu.SMEM((2, slot, 128), int32),
            pltpu.SMEM((par_lane, 128), int32),
            pltpu.VMEM((slot, k, kk), BF),
            pltpu.VMEM((slot, k, kk), BF),
            pltpu.VMEM((pool_size, k, kk), BF),
            pltpu.VMEM((pool_size, k, kk), BF),
            pltpu.VMEM((2, n_dev // 2, cap, k, kk), BF),
            pltpu.VMEM((2, n_dev // 2, cap, k, kk), BF),
            pltpu.VMEM((slot, k, kk), BF),
            pltpu.VMEM((slot, k, kk), BF),
            pltpu.VMEM(send_slots.shape, int32),
            pltpu.SMEM(send_slots.shape, int32),
            pltpu.VMEM((n_lane, par_lane, k, kk), F32),
            pltpu.VMEM((n_lane, par_lane, k, kk), F32),
            pltpu.VMEM((n_dev * par_lane + 1, k, kk), BF),
            pltpu.VMEM((n_lane, par_lane, k, kk), BF),
            pltpu.VMEM((4, kk, kk), BF),
            pltpu.VMEM((3, terms, PLANES * kk, kk), BF),
            pltpu.VMEM((terms, slot * k, PLANES * kk), BF),
            pltpu.VMEM((4, slot * k, kk), BF),
            dma((16,)),
            dma,
            dma,
            dma,
            dma,
            dma,
            dma,
            dma,
            dma,
            dma((2,)),
            dma((2,)),
            dma((3,)),
            dma((3,)),
        ],
        compiler_params=pltpu.CompilerParams(
            collective_id=0, has_side_effects=True, vmem_limit_bytes=56 * 1024 * 1024
        ),
    )(
        fine_in,
        counts.reshape(-1),
        neighbour_refs,
        offset_codes,
        neighbour_mask,
        send_slots,
        parent_of,
        child_code,
        coarse_refs,
        coarse_codes,
        coarse_mask,
        ops_x,
        ops_y,
        ops_z,
        filters,
    )


def solution(mesh):
    both = ("grp", "lane")
    in_specs = (
        P(None, both, None, None),
        P(None, both),
        P(None, both, None),
        P(None, both, None),
        P(None, both, None),
        P(None, both, None),
        P(both),
        P(both),
        P(both, None),
        P(both, None),
        P(both, None),
        P(),
        P(),
        P(),
        P(),
    )
    out_specs = (P(None, both, None, None), P(both, None, None))
    return jax.shard_map(body, mesh=mesh, in_specs=in_specs, out_specs=out_specs, check_vma=False)
```

```python
import functools

import jax
import jax.numpy as jnp
from jax import lax
from jax.experimental import pallas as pl
from jax.experimental.pallas import tpu as pltpu
from jax.sharding import PartitionSpec as P

MESH = pl.DeviceIdType.MESH
BF = jnp.bfloat16
F32 = jnp.float32
OFFSETS = 27
PLANES = 9
GROUP = 4


def dot_nn(a, b):
    return jnp.dot(a, b, preferred_element_type=F32)


def dot_nt(a, b):
    return lax.dot_general(a, b, (((1,), (1,)), ((), ())), preferred_element_type=F32)


def one_hot(shape, fn):
    rows = lax.broadcasted_iota(jnp.int32, shape, 0)
    cols = lax.broadcasted_iota(jnp.int32, shape, 1)
    return jnp.where(fn(rows, cols), 1.0, 0.0).astype(BF)


def spread_first(k):
    return one_hot((k, k * k), lambda i, j: (j >= i * k) & (j < i * k + k))


def spread_second(k):
    return one_hot((k, k * k), lambda i, j: lax.rem(j, k) == i)


def row_copies(left, k):
    return [jnp.broadcast_to(left[p : p + 1, :], left.shape).astype(BF) for p in range(k)]


def kron_store(out_ref, rows, right, k):
    for p in range(k):
        out_ref[p * k : (p + 1) * k, :] = rows[p] * right


def build_filters(filters_ref, hk_ref, k):
    first, second = spread_first(k), spread_second(k)
    right = [dot_nn(filters_ref[c], second).astype(BF) for c in range(2)]
    for cy in range(2):
        rows = row_copies(dot_nn(filters_ref[cy], first), k)
        for cz in range(2):
            kron_store(hk_ref.at[2 * cy + cz], rows, right[cz], k)


def build_tables(level, ops_y_ref, ops_z_ref, kr_ref, k, terms):
    first, second = spread_first(k), spread_second(k)
    eye = one_hot((k, k), lambda i, j: i == j)
    kk = k * k

    def turned(matrix):
        return dot_nt(eye, matrix).astype(BF)

    def one_term(m, carry):
        right = [dot_nn(turned(ops_z_ref[level, m, c]), second).astype(BF) for c in range(3)]
        for cy in range(3):
            rows = row_copies(dot_nn(turned(ops_y_ref[level, m, cy]), first), k)
            for cz in range(3):
                at = (3 * cy + cz) * kk
                kron_store(kr_ref.at[m, pl.ds(at, kk)], rows, right[cz], k)
        return carry

    lax.fori_loop(0, terms, one_term, 0)


def build_rows(level, ops_x_ref, group, k, terms):
    width = group * 3 * k
    blocks = []
    stacked = [
        jnp.concatenate([ops_x_ref[level, m, c] for m in range(terms)], axis=0) for c in range(3)
    ]
    for g in range(group):
        total = None
        for c in range(3):
            offset = (g * 3 + c) * k
            part = dot_nn(stacked[c], one_hot((k, width), lambda i, j: j == i + offset))
            total = part if total is None else total + part
        blocks.append(total.astype(BF))
    return jnp.concatenate(
        [blocks[g][m * k : (m + 1) * k] for m in range(terms) for g in range(group)], axis=0
    )


def spread_group(base, group, rows_mat, load, s_ref, k, terms):
    for plane in range(PLANES):
        source = jnp.concatenate(
            [load(base + g, 9 * c + plane) for g in range(group) for c in range(3)], axis=0
        )
        out = dot_nn(rows_mat, source).astype(BF)
        span = group * k
        for m in range(terms):
            s_ref[m, pl.ds(base * k, span), plane * k * k : (plane + 1) * k * k] = out[
                m * span : (m + 1) * span
            ]


def apply_tables(s_ref, kr_ref, rows, k, terms):
    def one_term(m, total):
        return total + dot_nn(s_ref[m, pl.ds(0, rows), :], kr_ref[m])

    return lax.fori_loop(0, terms, one_term, jnp.zeros((rows, k * k), F32))


def fill_index(refs, codes, mask, empty, out_ref, at):
    rows, slots = refs.shape
    code_of = lax.broadcasted_iota(jnp.int32, (rows, 128), 1)
    total = jnp.full((rows, 128), empty, jnp.int32)
    for j in range(slots):
        hit = (codes[:, j : j + 1] == code_of) & (mask[:, j : j + 1] == 1)
        total = jnp.where(hit, refs[:, j : j + 1], total)
    out_ref[at] = total


def tree_kernel(
    dims,
    fine_hbm,
    counts_hbm,
    refs_hbm,
    codes_hbm,
    mask_hbm,
    slots_hbm,
    parent_hbm,
    child_hbm,
    crefs_hbm,
    ccodes_hbm,
    cmask_hbm,
    ops_x_hbm,
    ops_y_hbm,
    ops_z_hbm,
    filters_hbm,
    out_ref,
    coarse_out,
    counts_ref,
    refs_ref,
    codes_ref,
    mask_ref,
    slots_ref,
    parent_ref,
    child_ref,
    crefs_ref,
    ccodes_ref,
    cmask_ref,
    ops_x_ref,
    ops_y_ref,
    ops_z_ref,
    filters_ref,
    idx_vec,
    cidx_vec,
    idx_ref,
    cidx_ref,
    own_0,
    own_1,
    pool_0,
    pool_1,
    packed_own,
    packed_mate,
    mate_0,
    mate_1,
    slots_vec,
    mate_slots,
    partial,
    rs_buf,
    coarse_all,
    group_all,
    hk,
    kr,
    s_buf,
    wide,
    in_sems,
    send_rs,
    recv_rs,
    send_ag,
    recv_ag,
    send_pass,
    recv_pass,
    send_co,
    recv_co,
    send_fine_sem,
    recv_fine,
    send_mate_sem,
    recv_mate,
):
    n_grp, n_lane, cap, slot, par_lane, k, terms = dims
    n_dev = n_grp * n_lane
    own, pool = (own_0, own_1), (pool_0, pool_1)
    mate_blocks = (mate_0, mate_1)
    grp = lax.axis_index("grp")
    lane = lax.axis_index("lane")
    me = grp * n_lane + lane

    def coords(d):
        return (lax.div(d, n_lane), lax.rem(d, n_lane))

    barrier = pltpu.get_barrier_semaphore()

    def greet(i, carry):
        pl.semaphore_signal(
            barrier, inc=1, device_id=coords(lax.rem(me + i, n_dev)), device_id_type=MESH
        )
        return carry

    fetches = [
        pltpu.make_async_copy(src, dst, in_sems.at[i])
        for i, (src, dst) in enumerate(
            [
                (filters_hbm, filters_ref),
                (fine_hbm.at[1], own_1),
                (child_hbm, child_ref),
                (parent_hbm, parent_ref),
                (slots_hbm, slots_ref),
                (fine_hbm.at[0], own_0),
                (crefs_hbm, crefs_ref),
                (ccodes_hbm, ccodes_ref),
                (cmask_hbm, cmask_ref),
                (ops_x_hbm, ops_x_ref),
                (ops_y_hbm, ops_y_ref),
                (ops_z_hbm, ops_z_ref),
                (refs_hbm, refs_ref),
                (codes_hbm, codes_ref),
                (mask_hbm, mask_ref),
                (counts_hbm, counts_ref),
            ]
        )
    ]
    for fetch in fetches:
        fetch.start()
    lax.fori_loop(1, n_dev, greet, 0)

    half = n_dev // 2
    lane_half = n_lane // 2
    side = lax.div(lane, lane_half)
    mate_lane = lax.rem(lane + lane_half, n_lane)
    mate = grp * n_lane + mate_lane
    place = grp * lane_half + lane - side * lane_half

    def peer(h):
        return lax.div(h, lane_half), side * lane_half + lax.rem(h, lane_half)

    def send_mate(src, dst, at):
        pltpu.make_async_remote_copy(
            src_ref=src,
            dst_ref=dst,
            send_sem=send_mate_sem.at[at],
            recv_sem=recv_mate.at[at],
            device_id=(grp, mate_lane),
            device_id_type=MESH,
        ).start()

    def send_fine(level, owner, blocks, slots, packed):
        def one(i, carry):
            h = lax.rem(place + i, half)
            to_grp, to_lane = peer(h)
            d = to_grp * n_lane + to_lane
            for c in range(cap):
                packed[level, h, c] = blocks[slots[level, 0, d * cap + c]]

            @pl.when(i > 0)
            def _():
                pltpu.make_async_remote_copy(
                    src_ref=packed.at[level, h],
                    dst_ref=pool[level].at[pl.ds(slot + owner * cap, cap)],
                    send_sem=send_fine_sem.at[level],
                    recv_sem=recv_fine.at[level],
                    device_id=(to_grp, to_lane),
                    device_id_type=MESH,
                ).start()

            return carry

        lax.fori_loop(0, half, one, 0)
        pool[level][pl.ds(slot + owner * cap, cap)] = packed[level, place]

    def pass_mate(level):
        await_bytes(mate_blocks[level], recv_mate.at[level])
        send_fine(level, mate, mate_blocks[level], mate_slots, packed_mate)

    def await_bytes(ref, sem):
        pltpu.make_async_copy(ref, ref, sem).wait()

    def keep_own(level):
        pool[level][slot + n_dev * cap] = jnp.zeros((k, k * k), BF)
        pool[level][pl.ds(0, slot)] = own[level][...]

    pl.semaphore_wait(barrier, n_dev - 1)
    send_mate(slots_hbm, slots_vec, 2)
    send_mate(fine_hbm.at[0], mate_0, 0)

    for fetch in fetches[:4]:
        fetch.wait()
    build_filters(filters_ref, hk, k)
    both = jnp.concatenate([filters_ref[0], filters_ref[1]], axis=0)
    for b in range(slot):
        lifted = dot_nn(both, own_1[b])
        code = child_ref[b]
        upper = code >= 4
        corner = jnp.where(upper, code - 4, code)
        chosen = jnp.where(upper, lifted[k:], lifted[:k])
        for c in range(4):
            wide[c, b * k : (b + 1) * k, :] = jnp.where(corner == c, chosen, 0.0).astype(BF)
    terms_up = dot_nt(wide[0], hk[0])
    for c in range(1, 4):
        terms_up = terms_up + dot_nt(wide[c], hk[c])
    for t in range(n_lane * par_lane):
        total = jnp.zeros((k, k * k), F32)
        for b in range(slot):
            total = total + jnp.where(parent_ref[b] == t, terms_up[b * k : (b + 1) * k], 0.0)
        partial[t // par_lane, t % par_lane] = total.astype(BF)

    def send_partial(i, carry):
        to = lax.rem(lane + i, n_lane)
        pltpu.make_async_remote_copy(
            src_ref=partial.at[to],
            dst_ref=rs_buf.at[lane],
            send_sem=send_rs,
            recv_sem=recv_rs,
            device_id=(grp, to),
            device_id_type=MESH,
        ).start()
        return carry

    lax.fori_loop(1, n_lane, send_partial, 0)
    send_mate(fine_hbm.at[1], mate_1, 1)
    await_bytes(slots_vec, recv_mate.at[2])
    slots_copy = pltpu.make_async_copy(slots_vec, mate_slots, in_sems.at[16])
    slots_copy.start()
    for fetch in fetches[4:6]:
        fetch.wait()
    send_fine(0, me, own_0, slots_ref, packed_own)
    slots_copy.wait()
    pass_mate(0)

    rs_buf[lane] = partial[lane]
    coarse_all[n_dev * par_lane] = jnp.zeros((k, k * k), BF)
    await_bytes(rs_buf.at[pl.ds(0, n_lane - 1)], recv_rs)
    total = rs_buf[0].astype(F32)
    for t in range(1, n_lane):
        total = total + rs_buf[t].astype(F32)
    coarse_all[pl.ds(me * par_lane, par_lane)] = total.astype(BF)

    odd = lax.rem(grp, 2)
    twin = grp + 1 - 2 * odd

    def send_coarse(i, carry):
        at = lax.rem(lax.div(grp, 2) * n_lane + lane + i, half)
        mine = coarse_all.at[pl.ds(me * par_lane, par_lane)]
        pltpu.make_async_remote_copy(
            src_ref=mine,
            dst_ref=mine,
            send_sem=send_ag,
            recv_sem=recv_ag,
            device_id=(2 * lax.div(at, n_lane) + odd, lax.rem(at, n_lane)),
            device_id_type=MESH,
        ).start()
        return carry

    lax.fori_loop(1, half, send_coarse, 0)
    send_fine(1, me, own_1, slots_ref, packed_own)
    keep_own(0)
    keep_own(1)
    for fetch in fetches[6:]:
        fetch.wait()
    fill_index(crefs_ref[...], ccodes_ref[...], cmask_ref[...], n_dev * par_lane, cidx_vec, ...)
    for level in range(2):
        fill_index(
            refs_ref[level], codes_ref[level], mask_ref[level], slot + n_dev * cap, idx_vec, level
        )
    table_copies = [
        pltpu.make_async_copy(cidx_vec, cidx_ref, in_sems.at[17]),
        pltpu.make_async_copy(idx_vec, idx_ref, in_sems.at[18]),
    ]
    for copy in table_copies:
        copy.start()
    for level in (0, 2):
        build_tables(level, ops_y_ref, ops_z_ref, kr.at[level], k, terms)

    pass_mate(1)
    build_tables(1, ops_y_ref, ops_z_ref, kr.at[1], k, terms)
    for copy in table_copies:
        copy.wait()

    await_bytes(coarse_all.at[pl.ds(0, (half - 1) * par_lane)], recv_ag)
    for pair in range(n_grp // 2):
        held = coarse_all.at[pl.ds((2 * pair + odd) * n_lane * par_lane, n_lane * par_lane)]
        pltpu.make_async_remote_copy(
            src_ref=held,
            dst_ref=held,
            send_sem=send_pass,
            recv_sem=recv_pass,
            device_id=(twin, lane),
            device_id_type=MESH,
        ).start()

    await_bytes(pool_0.at[pl.ds(0, (n_dev - 2) * cap)], recv_fine.at[0])
    result = fine_operator(0, pool_0, idx_ref, ops_x_ref, kr.at[0], s_buf, slot, k, terms)
    for b in range(slot):
        value = jnp.where(b < counts_ref[0], result[b * k : (b + 1) * k], 0.0)
        out_ref[0, b] = value.astype(BF)

    rows_mat = build_rows(2, ops_x_ref, 1, k, terms)
    await_bytes(coarse_all.at[pl.ds(0, half * par_lane)], recv_pass)
    for b in range(par_lane):
        spread_group(
            b, 1, rows_mat, lambda i, code: coarse_all[cidx_ref[i, code]], s_buf, k, terms
        )
    result = apply_tables(s_buf, kr.at[2], par_lane * k, k, terms).astype(BF)
    for b in range(par_lane):
        group_all[lane, b] = result[b * k : (b + 1) * k]
        coarse_out[b] = result[b * k : (b + 1) * k]

    def send_result(i, carry):
        to = lax.rem(lane + i, n_lane)
        pltpu.make_async_remote_copy(
            src_ref=group_all.at[lane],
            dst_ref=group_all.at[lane],
            send_sem=send_co,
            recv_sem=recv_co,
            device_id=(grp, to),
            device_id_type=MESH,
        ).start()
        return carry

    lax.fori_loop(1, n_lane, send_result, 0)

    await_bytes(pool_1.at[pl.ds(0, (n_dev - 2) * cap)], recv_fine.at[1])
    result = fine_operator(1, pool_1, idx_ref, ops_x_ref, kr.at[1], s_buf, slot, k, terms)
    await_bytes(group_all.at[pl.ds(0, n_lane - 1)], recv_co)
    correction = drop(
        group_all, parent_ref, child_ref, filters_ref, hk, wide, slot, par_lane, k
    )
    for b in range(slot):
        value = jnp.where(b < counts_ref[1], result[b * k : (b + 1) * k], 0.0)
        out_ref[1, b] = (value + correction[b * k : (b + 1) * k]).astype(BF)

    await_bytes(rs_buf.at[pl.ds(0, n_lane - 1)], send_rs)
    await_bytes(coarse_all.at[pl.ds(0, (half - 1) * par_lane)], send_ag)
    await_bytes(coarse_all.at[pl.ds(0, half * par_lane)], send_pass)
    await_bytes(group_all.at[pl.ds(0, n_lane - 1)], send_co)
    for level in range(2):
        await_bytes(pool[level].at[pl.ds(0, (n_dev - 2) * cap)], send_fine_sem.at[level])
        await_bytes(mate_blocks[level], send_mate_sem.at[level])
    await_bytes(slots_vec, send_mate_sem.at[2])


def fine_operator(level, pool, idx_ref, ops_x_ref, kr, s_buf, slot, k, terms):
    group = GROUP if slot % GROUP == 0 else 1
    rows_mat = build_rows(level, ops_x_ref, group, k, terms)

    def one_group(g, carry):
        spread_group(
            pl.multiple_of(g * group, group),
            group,
            rows_mat,
            lambda i, code: pool[idx_ref[level, i, code]],
            s_buf,
            k,
            terms,
        )
        return carry

    lax.fori_loop(0, slot // group, one_group, 0)
    return apply_tables(s_buf, kr, slot * k, k, terms)


def drop(group_all, parent_ref, child_ref, filters_ref, hk, wide, slot, par_lane, k):
    eye = one_hot((k, k), lambda i, j: i == j)
    both = jnp.concatenate([dot_nt(eye, filters_ref[c]).astype(BF) for c in range(2)], axis=0)
    for b in range(slot):
        parent = parent_ref[b]
        held = jnp.maximum(parent, 0)
        lowered = dot_nn(both, group_all[held // par_lane, held % par_lane] if par_lane > 1 else group_all[held, 0])
        code = child_ref[b]
        upper = code >= 4
        corner = jnp.where(upper, code - 4, code)
        corner = jnp.where(parent >= 0, corner, -1)
        chosen = jnp.where(upper, lowered[k:], lowered[:k])
        for c in range(4):
            wide[c, b * k : (b + 1) * k, :] = jnp.where(corner == c, chosen, 0.0).astype(BF)
    total = dot_nn(wide[0], hk[0])
    for c in range(1, 4):
        total = total + dot_nn(wide[c], hk[c])
    return total


def body(
    fine_in,
    counts,
    neighbour_refs,
    offset_codes,
    neighbour_mask,
    send_slots,
    parent_of,
    child_code,
    coarse_refs,
    coarse_codes,
    coarse_mask,
    ops_x,
    ops_y,
    ops_z,
    filters,
):
    n_grp, n_lane = lax.axis_size("grp"), lax.axis_size("lane")
    n_dev = n_grp * n_lane
    k = filters.shape[1]
    kk = k * k
    slot = fine_in.shape[1]
    cap = send_slots.shape[2] // n_dev
    par_lane = coarse_refs.shape[0]
    terms = ops_x.shape[1]
    dims = (n_grp, n_lane, cap, slot, par_lane, k, terms)
    pool_size = slot + n_dev * cap + 1
    int32 = jnp.int32
    vmem = pl.BlockSpec(memory_space=pltpu.VMEM)
    hbm = pl.BlockSpec(memory_space=pl.ANY)
    dma = pltpu.SemaphoreType.DMA
    return pl.pallas_call(
        functools.partial(tree_kernel, dims),
        out_shape=(
            pltpu.VMEM(fine_in.shape, BF),
            pltpu.VMEM((par_lane, k, kk), BF),
        ),
        in_specs=[hbm] * 15,
        out_specs=(vmem, vmem),
        scratch_shapes=[
            pltpu.SMEM((2,), int32),
            pltpu.VMEM(neighbour_refs.shape, int32),
            pltpu.VMEM(offset_codes.shape, int32),
            pltpu.VMEM(neighbour_mask.shape, int32),
            pltpu.SMEM(send_slots.shape, int32),
            pltpu.SMEM(parent_of.shape, int32),
            pltpu.SMEM(child_code.shape, int32),
            pltpu.VMEM(coarse_refs.shape, int32),
            pltpu.VMEM(coarse_codes.shape, int32),
            pltpu.VMEM(coarse_mask.shape, int32),
            pltpu.VMEM(ops_x.shape, BF),
            pltpu.VMEM(ops_y.shape, BF),
            pltpu.VMEM(ops_z.shape, BF),
            pltpu.VMEM(filters.shape, BF),
            pltpu.VMEM((2, slot, 128), int32),
            pltpu.VMEM((par_lane, 128), int32),
            pltpu.SMEM((2, slot, 128), int32),
            pltpu.SMEM((par_lane, 128), int32),
            pltpu.VMEM((slot, k, kk), BF),
            pltpu.VMEM((slot, k, kk), BF),
            pltpu.VMEM((pool_size, k, kk), BF),
            pltpu.VMEM((pool_size, k, kk), BF),
            pltpu.VMEM((2, n_dev // 2, cap, k, kk), BF),
            pltpu.VMEM((2, n_dev // 2, cap, k, kk), BF),
            pltpu.VMEM((slot, k, kk), BF),
            pltpu.VMEM((slot, k, kk), BF),
            pltpu.VMEM(send_slots.shape, int32),
            pltpu.SMEM(send_slots.shape, int32),
            pltpu.VMEM((n_lane, par_lane, k, kk), BF),
            pltpu.VMEM((n_lane, par_lane, k, kk), BF),
            pltpu.VMEM((n_dev * par_lane + 1, k, kk), BF),
            pltpu.VMEM((n_lane, par_lane, k, kk), BF),
            pltpu.VMEM((4, kk, kk), BF),
            pltpu.VMEM((3, terms, PLANES * kk, kk), BF),
            pltpu.VMEM((terms, slot * k, PLANES * kk), BF),
            pltpu.VMEM((4, slot * k, kk), BF),
            dma((20,)),
            dma,
            dma,
            dma,
            dma,
            dma,
            dma,
            dma,
            dma,
            dma((2,)),
            dma((2,)),
            dma((3,)),
            dma((3,)),
        ],
        compiler_params=pltpu.CompilerParams(
            collective_id=0, has_side_effects=True, vmem_limit_bytes=56 * 1024 * 1024
        ),
    )(
        fine_in,
        counts.reshape(-1),
        neighbour_refs,
        offset_codes,
        neighbour_mask,
        send_slots,
        parent_of,
        child_code,
        coarse_refs,
        coarse_codes,
        coarse_mask,
        ops_x,
        ops_y,
        ops_z,
        filters,
    )


def solution(mesh):
    both = ("grp", "lane")
    in_specs = (
        P(None, both, None, None),
        P(None, both),
        P(None, both, None),
        P(None, both, None),
        P(None, both, None),
        P(None, both, None),
        P(both),
        P(both),
        P(both, None),
        P(both, None),
        P(both, None),
        P(),
        P(),
        P(),
        P(),
    )
    out_specs = (P(None, both, None, None), P(both, None, None))
    return jax.shard_map(body, mesh=mesh, in_specs=in_specs, out_specs=out_specs, check_vma=False)
```

```python
import functools

import jax
import jax.numpy as jnp
from jax import lax
from jax.experimental import pallas as pl
from jax.experimental.pallas import tpu as pltpu
from jax.sharding import PartitionSpec as P

MESH = pl.DeviceIdType.MESH
BF = jnp.bfloat16
F32 = jnp.float32
OFFSETS = 27
PLANES = 9
GROUP = 4


def dot_nn(a, b):
    return jnp.dot(a, b, preferred_element_type=F32)


def dot_nt(a, b):
    return lax.dot_general(a, b, (((1,), (1,)), ((), ())), preferred_element_type=F32)


def one_hot(shape, fn):
    rows = lax.broadcasted_iota(jnp.int32, shape, 0)
    cols = lax.broadcasted_iota(jnp.int32, shape, 1)
    return jnp.where(fn(rows, cols), 1.0, 0.0).astype(BF)


def spread_first(k):
    return one_hot((k, k * k), lambda i, j: (j >= i * k) & (j < i * k + k))


def spread_second(k):
    return one_hot((k, k * k), lambda i, j: lax.rem(j, k) == i)


def row_copies(left, k):
    return [jnp.broadcast_to(left[p : p + 1, :], left.shape).astype(BF) for p in range(k)]


def kron_store(out_ref, rows, right, k):
    for p in range(k):
        out_ref[p * k : (p + 1) * k, :] = rows[p] * right


def build_filters(filters_ref, hk_ref, k):
    first, second = spread_first(k), spread_second(k)
    right = [dot_nn(filters_ref[c], second).astype(BF) for c in range(2)]
    for cy in range(2):
        rows = row_copies(dot_nn(filters_ref[cy], first), k)
        for cz in range(2):
            kron_store(hk_ref.at[2 * cy + cz], rows, right[cz], k)


def build_tables(level, ops_y_ref, ops_z_ref, kr_ref, k, terms):
    first, second = spread_first(k), spread_second(k)
    eye = one_hot((k, k), lambda i, j: i == j)
    kk = k * k

    def turned(matrix):
        return dot_nt(eye, matrix).astype(BF)

    def one_term(m, carry):
        right = [dot_nn(turned(ops_z_ref[level, m, c]), second).astype(BF) for c in range(3)]
        for cy in range(3):
            rows = row_copies(dot_nn(turned(ops_y_ref[level, m, cy]), first), k)
            for cz in range(3):
                at = (3 * cy + cz) * kk
                kron_store(kr_ref.at[m, pl.ds(at, kk)], rows, right[cz], k)
        return carry

    lax.fori_loop(0, terms, one_term, 0)


def build_rows(level, ops_x_ref, group, k, terms):
    width = group * 3 * k
    blocks = []
    stacked = [
        jnp.concatenate([ops_x_ref[level, m, c] for m in range(terms)], axis=0) for c in range(3)
    ]
    for g in range(group):
        total = None
        for c in range(3):
            offset = (g * 3 + c) * k
            part = dot_nn(stacked[c], one_hot((k, width), lambda i, j: j == i + offset))
            total = part if total is None else total + part
        blocks.append(total.astype(BF))
    return jnp.concatenate(
        [blocks[g][m * k : (m + 1) * k] for m in range(terms) for g in range(group)], axis=0
    )


def spread_group(base, group, rows_mat, load, s_ref, k, terms):
    for plane in range(PLANES):
        source = jnp.concatenate(
            [load(base + g, 9 * c + plane) for g in range(group) for c in range(3)], axis=0
        )
        out = dot_nn(rows_mat, source).astype(BF)
        span = group * k
        for m in range(terms):
            s_ref[m, pl.ds(base * k, span), plane * k * k : (plane + 1) * k * k] = out[
                m * span : (m + 1) * span
            ]


def apply_tables(s_ref, kr_ref, rows, k, terms):
    def one_term(m, total):
        return total + dot_nn(s_ref[m, pl.ds(0, rows), :], kr_ref[m])

    return lax.fori_loop(0, terms, one_term, jnp.zeros((rows, k * k), F32))


def fill_index(refs, codes, mask, empty, out_ref, at):
    rows, slots = refs.shape
    code_of = lax.broadcasted_iota(jnp.int32, (rows, 128), 1)
    total = jnp.full((rows, 128), empty, jnp.int32)
    for j in range(slots):
        hit = (codes[:, j : j + 1] == code_of) & (mask[:, j : j + 1] == 1)
        total = jnp.where(hit, refs[:, j : j + 1], total)
    out_ref[at] = total


def tree_kernel(
    dims,
    fine_hbm,
    counts_hbm,
    refs_hbm,
    codes_hbm,
    mask_hbm,
    slots_hbm,
    parent_hbm,
    child_hbm,
    crefs_hbm,
    ccodes_hbm,
    cmask_hbm,
    ops_x_hbm,
    ops_y_hbm,
    ops_z_hbm,
    filters_hbm,
    out_ref,
    coarse_out,
    counts_ref,
    refs_ref,
    codes_ref,
    mask_ref,
    slots_ref,
    parent_ref,
    child_ref,
    crefs_ref,
    ccodes_ref,
    cmask_ref,
    ops_x_ref,
    ops_y_ref,
    ops_z_ref,
    filters_ref,
    idx_vec,
    cidx_vec,
    idx_ref,
    cidx_ref,
    own_0,
    own_1,
    pool_0,
    pool_1,
    packed_own,
    packed_mate,
    mate_0,
    mate_1,
    slots_vec,
    mate_slots,
    partial,
    rs_buf,
    coarse_all,
    group_all,
    hk,
    kr,
    s_buf,
    wide,
    drop_buf,
    in_sems,
    send_rs,
    recv_rs,
    send_ag,
    recv_ag,
    send_pass,
    recv_pass,
    send_co,
    recv_co,
    send_fine_sem,
    recv_fine,
    send_mate_sem,
    recv_mate,
):
    n_grp, n_lane, cap, slot, par_lane, k, terms = dims
    n_dev = n_grp * n_lane
    own, pool = (own_0, own_1), (pool_0, pool_1)
    mate_blocks = (mate_0, mate_1)
    grp = lax.axis_index("grp")
    lane = lax.axis_index("lane")
    me = grp * n_lane + lane

    def coords(d):
        return (lax.div(d, n_lane), lax.rem(d, n_lane))

    barrier = pltpu.get_barrier_semaphore()

    def greet(i, carry):
        pl.semaphore_signal(
            barrier, inc=1, device_id=coords(lax.rem(me + i, n_dev)), device_id_type=MESH
        )
        return carry

    fetches = [
        pltpu.make_async_copy(src, dst, in_sems.at[i])
        for i, (src, dst) in enumerate(
            [
                (filters_hbm, filters_ref),
                (fine_hbm.at[1], own_1),
                (child_hbm, child_ref),
                (parent_hbm, parent_ref),
                (slots_hbm, slots_ref),
                (fine_hbm.at[0], own_0),
                (crefs_hbm, crefs_ref),
                (ccodes_hbm, ccodes_ref),
                (cmask_hbm, cmask_ref),
                (ops_x_hbm, ops_x_ref),
                (ops_y_hbm, ops_y_ref),
                (ops_z_hbm, ops_z_ref),
                (refs_hbm, refs_ref),
                (codes_hbm, codes_ref),
                (mask_hbm, mask_ref),
                (counts_hbm, counts_ref),
            ]
        )
    ]
    for fetch in fetches:
        fetch.start()
    lax.fori_loop(1, n_dev, greet, 0)

    half = n_dev // 2
    lane_half = n_lane // 2
    side = lax.div(lane, lane_half)
    mate_lane = lax.rem(lane + lane_half, n_lane)
    mate = grp * n_lane + mate_lane
    place = grp * lane_half + lane - side * lane_half

    def peer(h):
        return lax.div(h, lane_half), side * lane_half + lax.rem(h, lane_half)

    def send_mate(src, dst, at):
        pltpu.make_async_remote_copy(
            src_ref=src,
            dst_ref=dst,
            send_sem=send_mate_sem.at[at],
            recv_sem=recv_mate.at[at],
            device_id=(grp, mate_lane),
            device_id_type=MESH,
        ).start()

    def send_fine(level, owner, blocks, slots, packed):
        def one(i, carry):
            h = lax.rem(place + i, half)
            to_grp, to_lane = peer(h)
            d = to_grp * n_lane + to_lane
            for c in range(cap):
                packed[level, h, c] = blocks[slots[level, 0, d * cap + c]]

            @pl.when(i > 0)
            def _():
                pltpu.make_async_remote_copy(
                    src_ref=packed.at[level, h],
                    dst_ref=pool[level].at[pl.ds(slot + owner * cap, cap)],
                    send_sem=send_fine_sem.at[level],
                    recv_sem=recv_fine.at[level],
                    device_id=(to_grp, to_lane),
                    device_id_type=MESH,
                ).start()

            return carry

        lax.fori_loop(0, half, one, 0)
        pool[level][pl.ds(slot + owner * cap, cap)] = packed[level, place]

    def pass_mate(level):
        await_bytes(mate_blocks[level], recv_mate.at[level])
        send_fine(level, mate, mate_blocks[level], mate_slots, packed_mate)

    def await_bytes(ref, sem):
        pltpu.make_async_copy(ref, ref, sem).wait()

    def keep_own(level):
        pool[level][slot + n_dev * cap] = jnp.zeros((k, k * k), BF)
        pool[level][pl.ds(0, slot)] = own[level][...]

    fetches[0].wait()
    build_filters(filters_ref, hk, k)
    pl.semaphore_wait(barrier, n_dev - 1)
    send_mate(slots_hbm, slots_vec, 2)
    send_mate(fine_hbm.at[0], mate_0, 0)

    for fetch in fetches[1:4]:
        fetch.wait()
    both = jnp.concatenate([filters_ref[0], filters_ref[1]], axis=0)
    for b in range(slot):
        lifted = dot_nn(both, own_1[b])
        code = child_ref[b]
        upper = code >= 4
        corner = jnp.where(upper, code - 4, code)
        chosen = jnp.where(upper, lifted[k:], lifted[:k])
        for c in range(4):
            wide[c, b * k : (b + 1) * k, :] = jnp.where(corner == c, chosen, 0.0).astype(BF)
    terms_up = dot_nt(wide[0], hk[0])
    for c in range(1, 4):
        terms_up = terms_up + dot_nt(wide[c], hk[c])
    for t in range(n_lane * par_lane):
        total = jnp.zeros((k, k * k), F32)
        for b in range(slot):
            total = total + jnp.where(parent_ref[b] == t, terms_up[b * k : (b + 1) * k], 0.0)
        partial[t // par_lane, t % par_lane] = total

    def send_partial(i, carry):
        to = lax.rem(lane + i, n_lane)
        pltpu.make_async_remote_copy(
            src_ref=partial.at[to],
            dst_ref=rs_buf.at[lane],
            send_sem=send_rs,
            recv_sem=recv_rs,
            device_id=(grp, to),
            device_id_type=MESH,
        ).start()
        return carry

    lax.fori_loop(1, n_lane, send_partial, 0)
    send_mate(fine_hbm.at[1], mate_1, 1)
    await_bytes(slots_vec, recv_mate.at[2])
    slots_copy = pltpu.make_async_copy(slots_vec, mate_slots, in_sems.at[16])
    slots_copy.start()
    for fetch in fetches[4:6]:
        fetch.wait()
    send_fine(0, me, own_0, slots_ref, packed_own)
    slots_copy.wait()
    pass_mate(0)

    rs_buf[lane] = partial[lane]
    coarse_all[n_dev * par_lane] = jnp.zeros((k, k * k), BF)
    await_bytes(rs_buf.at[pl.ds(0, n_lane - 1)], recv_rs)
    total = rs_buf[0]
    for t in range(1, n_lane):
        total = total + rs_buf[t]
    coarse_all[pl.ds(me * par_lane, par_lane)] = total.astype(BF)

    odd = lax.rem(grp, 2)
    twin = grp + 1 - 2 * odd

    def send_coarse(i, carry):
        at = lax.rem(lax.div(grp, 2) * n_lane + lane + i, half)
        mine = coarse_all.at[pl.ds(me * par_lane, par_lane)]
        pltpu.make_async_remote_copy(
            src_ref=mine,
            dst_ref=mine,
            send_sem=send_ag,
            recv_sem=recv_ag,
            device_id=(2 * lax.div(at, n_lane) + odd, lax.rem(at, n_lane)),
            device_id_type=MESH,
        ).start()
        return carry

    lax.fori_loop(1, half, send_coarse, 0)
    send_fine(1, me, own_1, slots_ref, packed_own)
    keep_own(0)
    keep_own(1)
    for fetch in fetches[6:]:
        fetch.wait()
    fill_index(crefs_ref[...], ccodes_ref[...], cmask_ref[...], n_dev * par_lane, cidx_vec, ...)
    for level in range(2):
        fill_index(
            refs_ref[level], codes_ref[level], mask_ref[level], slot + n_dev * cap, idx_vec, level
        )
    table_copies = [
        pltpu.make_async_copy(cidx_vec, cidx_ref, in_sems.at[17]),
        pltpu.make_async_copy(idx_vec, idx_ref, in_sems.at[18]),
    ]
    for copy in table_copies:
        copy.start()
    for level in (0, 2):
        build_tables(level, ops_y_ref, ops_z_ref, kr.at[level], k, terms)

    pass_mate(1)

    await_bytes(coarse_all.at[pl.ds(0, (half - 1) * par_lane)], recv_ag)
    for pair in range(n_grp // 2):
        held = coarse_all.at[pl.ds((2 * pair + odd) * n_lane * par_lane, n_lane * par_lane)]
        pltpu.make_async_remote_copy(
            src_ref=held,
            dst_ref=held,
            send_sem=send_pass,
            recv_sem=recv_pass,
            device_id=(twin, lane),
            device_id_type=MESH,
        ).start()

    build_tables(1, ops_y_ref, ops_z_ref, kr.at[1], k, terms)
    for copy in table_copies:
        copy.wait()
    rows_mat = build_rows(2, ops_x_ref, 1, k, terms)
    await_bytes(coarse_all.at[pl.ds(0, half * par_lane)], recv_pass)
    for b in range(par_lane):
        spread_group(
            b, 1, rows_mat, lambda i, code: coarse_all[cidx_ref[i, code]], s_buf, k, terms
        )
    result = apply_tables(s_buf, kr.at[2], par_lane * k, k, terms).astype(BF)
    for b in range(par_lane):
        group_all[lane, b] = result[b * k : (b + 1) * k]
        coarse_out[b] = result[b * k : (b + 1) * k]

    def send_result(i, carry):
        to = lax.rem(lane + i, n_lane)
        pltpu.make_async_remote_copy(
            src_ref=group_all.at[lane],
            dst_ref=group_all.at[lane],
            send_sem=send_co,
            recv_sem=recv_co,
            device_id=(grp, to),
            device_id_type=MESH,
        ).start()
        return carry

    lax.fori_loop(1, n_lane, send_result, 0)

    await_bytes(pool_0.at[pl.ds(0, (n_dev - 2) * cap)], recv_fine.at[0])
    result = fine_operator(0, pool_0, idx_ref, ops_x_ref, kr.at[0], s_buf, slot, k, terms)
    for b in range(slot):
        value = jnp.where(b < counts_ref[0], result[b * k : (b + 1) * k], 0.0)
        out_ref[0, b] = value.astype(BF)

    await_bytes(group_all.at[pl.ds(0, n_lane - 1)], recv_co)
    correction = drop(
        group_all, parent_ref, child_ref, filters_ref, hk, wide, slot, par_lane, k
    )
    drop_buf[...] = correction
    await_bytes(pool_1.at[pl.ds(0, (n_dev - 2) * cap)], recv_fine.at[1])
    result = fine_operator(1, pool_1, idx_ref, ops_x_ref, kr.at[1], s_buf, slot, k, terms)
    for b in range(slot):
        value = jnp.where(b < counts_ref[1], result[b * k : (b + 1) * k], 0.0)
        out_ref[1, b] = (value + drop_buf[b * k : (b + 1) * k, :]).astype(BF)

    await_bytes(rs_buf.at[pl.ds(0, n_lane - 1)], send_rs)
    await_bytes(coarse_all.at[pl.ds(0, (half - 1) * par_lane)], send_ag)
    await_bytes(coarse_all.at[pl.ds(0, half * par_lane)], send_pass)
    await_bytes(group_all.at[pl.ds(0, n_lane - 1)], send_co)
    for level in range(2):
        await_bytes(pool[level].at[pl.ds(0, (n_dev - 2) * cap)], send_fine_sem.at[level])
        await_bytes(mate_blocks[level], send_mate_sem.at[level])
    await_bytes(slots_vec, send_mate_sem.at[2])


def fine_operator(level, pool, idx_ref, ops_x_ref, kr, s_buf, slot, k, terms):
    group = GROUP if slot % GROUP == 0 else 1
    rows_mat = build_rows(level, ops_x_ref, group, k, terms)

    def one_group(g, carry):
        spread_group(
            pl.multiple_of(g * group, group),
            group,
            rows_mat,
            lambda i, code: pool[idx_ref[level, i, code]],
            s_buf,
            k,
            terms,
        )
        return carry

    lax.fori_loop(0, slot // group, one_group, 0)
    return apply_tables(s_buf, kr, slot * k, k, terms)


def drop(group_all, parent_ref, child_ref, filters_ref, hk, wide, slot, par_lane, k):
    eye = one_hot((k, k), lambda i, j: i == j)
    both = jnp.concatenate([dot_nt(eye, filters_ref[c]).astype(BF) for c in range(2)], axis=0)
    for b in range(slot):
        parent = parent_ref[b]
        held = jnp.maximum(parent, 0)
        lowered = dot_nn(both, group_all[held // par_lane, held % par_lane] if par_lane > 1 else group_all[held, 0])
        code = child_ref[b]
        upper = code >= 4
        corner = jnp.where(upper, code - 4, code)
        corner = jnp.where(parent >= 0, corner, -1)
        chosen = jnp.where(upper, lowered[k:], lowered[:k])
        for c in range(4):
            wide[c, b * k : (b + 1) * k, :] = jnp.where(corner == c, chosen, 0.0).astype(BF)
    total = dot_nn(wide[0], hk[0])
    for c in range(1, 4):
        total = total + dot_nn(wide[c], hk[c])
    return total


def body(
    fine_in,
    counts,
    neighbour_refs,
    offset_codes,
    neighbour_mask,
    send_slots,
    parent_of,
    child_code,
    coarse_refs,
    coarse_codes,
    coarse_mask,
    ops_x,
    ops_y,
    ops_z,
    filters,
):
    n_grp, n_lane = lax.axis_size("grp"), lax.axis_size("lane")
    n_dev = n_grp * n_lane
    k = filters.shape[1]
    kk = k * k
    slot = fine_in.shape[1]
    cap = send_slots.shape[2] // n_dev
    par_lane = coarse_refs.shape[0]
    terms = ops_x.shape[1]
    dims = (n_grp, n_lane, cap, slot, par_lane, k, terms)
    pool_size = slot + n_dev * cap + 1
    int32 = jnp.int32
    vmem = pl.BlockSpec(memory_space=pltpu.VMEM)
    hbm = pl.BlockSpec(memory_space=pl.ANY)
    dma = pltpu.SemaphoreType.DMA
    return pl.pallas_call(
        functools.partial(tree_kernel, dims),
        out_shape=(
            pltpu.VMEM(fine_in.shape, BF),
            pltpu.VMEM((par_lane, k, kk), BF),
        ),
        in_specs=[hbm] * 15,
        out_specs=(vmem, vmem),
        scratch_shapes=[
            pltpu.SMEM((2,), int32),
            pltpu.VMEM(neighbour_refs.shape, int32),
            pltpu.VMEM(offset_codes.shape, int32),
            pltpu.VMEM(neighbour_mask.shape, int32),
            pltpu.SMEM(send_slots.shape, int32),
            pltpu.SMEM(parent_of.shape, int32),
            pltpu.SMEM(child_code.shape, int32),
            pltpu.VMEM(coarse_refs.shape, int32),
            pltpu.VMEM(coarse_codes.shape, int32),
            pltpu.VMEM(coarse_mask.shape, int32),
            pltpu.VMEM(ops_x.shape, BF),
            pltpu.VMEM(ops_y.shape, BF),
            pltpu.VMEM(ops_z.shape, BF),
            pltpu.VMEM(filters.shape, BF),
            pltpu.VMEM((2, slot, 128), int32),
            pltpu.VMEM((par_lane, 128), int32),
            pltpu.SMEM((2, slot, 128), int32),
            pltpu.SMEM((par_lane, 128), int32),
            pltpu.VMEM((slot, k, kk), BF),
            pltpu.VMEM((slot, k, kk), BF),
            pltpu.VMEM((pool_size, k, kk), BF),
            pltpu.VMEM((pool_size, k, kk), BF),
            pltpu.VMEM((2, n_dev // 2, cap, k, kk), BF),
            pltpu.VMEM((2, n_dev // 2, cap, k, kk), BF),
            pltpu.VMEM((slot, k, kk), BF),
            pltpu.VMEM((slot, k, kk), BF),
            pltpu.VMEM(send_slots.shape, int32),
            pltpu.SMEM(send_slots.shape, int32),
            pltpu.VMEM((n_lane, par_lane, k, kk), F32),
            pltpu.VMEM((n_lane, par_lane, k, kk), F32),
            pltpu.VMEM((n_dev * par_lane + 1, k, kk), BF),
            pltpu.VMEM((n_lane, par_lane, k, kk), BF),
            pltpu.VMEM((4, kk, kk), BF),
            pltpu.VMEM((3, terms, PLANES * kk, kk), BF),
            pltpu.VMEM((terms, slot * k, PLANES * kk), BF),
            pltpu.VMEM((4, slot * k, kk), BF),
            pltpu.VMEM((slot * k, kk), F32),
            dma((20,)),
            dma,
            dma,
            dma,
            dma,
            dma,
            dma,
            dma,
            dma,
            dma((2,)),
            dma((2,)),
            dma((3,)),
            dma((3,)),
        ],
        compiler_params=pltpu.CompilerParams(
            collective_id=0, has_side_effects=True, vmem_limit_bytes=56 * 1024 * 1024
        ),
    )(
        fine_in,
        counts.reshape(-1),
        neighbour_refs,
        offset_codes,
        neighbour_mask,
        send_slots,
        parent_of,
        child_code,
        coarse_refs,
        coarse_codes,
        coarse_mask,
        ops_x,
        ops_y,
        ops_z,
        filters,
    )


def solution(mesh):
    both = ("grp", "lane")
    in_specs = (
        P(None, both, None, None),
        P(None, both),
        P(None, both, None),
        P(None, both, None),
        P(None, both, None),
        P(None, both, None),
        P(both),
        P(both),
        P(both, None),
        P(both, None),
        P(both, None),
        P(),
        P(),
        P(),
        P(),
    )
    out_specs = (P(None, both, None, None), P(both, None, None))
    return jax.shard_map(body, mesh=mesh, in_specs=in_specs, out_specs=out_specs, check_vma=False)
```
